32 devices in a mesh: groups: 2 (over x), seq: 8 (over z, y), head: 2 (over core).
Axes of the slice: x: 2, y: 2, z: 4, core: 2. Of those that a mesh axis runs over, the one named last changes fastest.
Arguments:
- queries: bfloat16 [16384, 1536], P(('groups', 'seq', 'head')), parts along dimension 0, may hold values from -5 to 5
- keys: bfloat16 [16384, 1536], P(('groups', 'seq', 'head')), parts along dimension 0, may hold values from -5 to 5
- values: bfloat16 [16384, 1536], P(('groups', 'seq', 'head')), parts along dimension 0, may hold values from -6 to 6
- tile_lists: int32 [256, 24], P('groups'), parts along dimension 0, may hold values from 0 to 127, as said below
Outputs:
- attended: bfloat16 [16384, 1536], P(('groups', 'seq', 'head')), parts along dimension 0
The draws below stay inside these ranges and needn't reach their ends.
There are 2 independent parts, one for each index of `groups`. The reference program is written for one: setup_inputs(seed, part) draws one part's arguments, and reference() takes and returns one part's arrays. A program takes and returns all parts, laid end to end along the dimension named above; each array names one. Nothing has to cross between parts.
Inputs may be any that keep to these rules, and one draw needn't show every extreme that they name: `tile_lists`: each row names 24 distinct tiles. Cut the tiles into runs of 16 consecutive ones: the rows of one run together name at most 8 distinct tiles of any run, exactly 8 tiles of half of the runs and 4 of the others.
All inputs are finite; a program needn't handle non-finite values.
Results may differ from the reference program's by a relative error of at most 0.0042.
Values may be sent and summed in bfloat16 or wider, within the bound.
No kernel may reach another device: no remote copies, remote signals or barrier semaphores. Data moves between devices by JAX's collectives and lax.ppermute only.
A program may use at most 128 MiB of HBM per device.

```python
import math
import jax
import jax.numpy as jnp
from jax import lax

HEADS = 12
HD = 128
TILE = 64
TOPK = 24
TOKENS = 8192
NTILES = 128
SHARD_TILES = 16
CAP = 8


def make_lists(key):
    key = jax.random.fold_in(key, 55)
    run_count = NTILES // SHARD_TILES
    union_size = 3 * run_count * CAP // 4
    step_size = -(-union_size // SHARD_TILES)

    def one_run(run_key):
        perm_key, tile_key, order_key = jax.random.split(run_key, 3)
        source_rank = jax.random.permutation(perm_key, run_count)
        counts = jnp.where(source_rank < run_count // 2, CAP, CAP // 2)
        raw_scores = jax.random.randint(tile_key, (run_count, SHARD_TILES), 0, 1 << 20) * SHARD_TILES
        raw_scores = raw_scores + jnp.arange(SHARD_TILES, dtype=jnp.int32)[None, :]
        tile_ranks = jnp.argsort(jnp.argsort(raw_scores, axis=1), axis=1)
        chosen = (tile_ranks < counts[:, None]).reshape(-1)
        union_tiles = jnp.argsort(jnp.where(chosen, 0, 1), stable=True)[:union_size]
        union_tiles = union_tiles[jax.random.permutation(order_key, union_size)]
        starts = jnp.arange(SHARD_TILES)[:, None] * step_size + jnp.arange(TOPK)[None, :]
        return union_tiles[starts % union_size]
    run_keys = jax.random.split(key, run_count)
    return jax.vmap(one_run)(run_keys).reshape(NTILES, TOPK).astype(jnp.int32)


def draw_tile_lists(key, part):
    return make_lists(key)


def draw_queries(key, part):
    key = jax.random.fold_in(key, 2)
    result = jnp.clip(jax.random.normal(key, (TOKENS, HEADS * HD)), -4.0, 4.0)
    return result.astype(jnp.bfloat16)


def draw_keys(key, part):
    key = jax.random.fold_in(key, 3)
    scale_key, body_key = jax.random.split(key, 2)
    row_scale = jnp.exp(jax.random.uniform(scale_key, (TOKENS, 1), minval=math.log(0.15), maxval=math.log(1.5)))
    result = row_scale * jnp.clip(jax.random.normal(body_key, (TOKENS, HEADS * HD)), -3.0, 3.0)
    return result.astype(jnp.bfloat16)


def level_of(key, shape, cuts, low, top_value):
    def one(axis_at, parts):
        draws = jax.random.uniform(jax.random.fold_in(jax.random.fold_in(key, 6), axis_at), (parts,), jnp.float32, low / len(cuts), top_value / len(cuts))
        return jnp.repeat(jnp.exp(draws), shape[axis_at] // parts).reshape((-1,) + (1,) * (len(shape) - axis_at - 1))

    level = one(*cuts[0])
    for cut in cuts[1:]:
        level = level * one(*cut)
    return level


def gaussian(rng, dims, width, bound, cuts=(), held_as=jnp.bfloat16):
    drawn = jax.random.normal(rng, dims, jnp.float32) * width
    if len(cuts) > 0:
        drawn = level_of(rng, dims, cuts, -0.22, 0.18) * drawn
    return jnp.clip(drawn, min=-bound, max=bound).astype(held_as)


def setup_inputs(seed: int = 0, part: int = 0) -> dict:
    key_list = jax.random.split(jax.random.key(seed), 5)
    part_splits = jax.random.split(jax.random.fold_in(key_list[4], part), 5)
    queries = draw_queries(jax.random.fold_in(jax.random.fold_in(key_list[4], part), 71), part)
    keys = draw_keys(jax.random.fold_in(jax.random.fold_in(key_list[4], part), 71), part)
    values = gaussian(part_splits[2], (TOKENS, HEADS * HD), 1.0, 6.0, ((0, 16),))
    tile_lists = draw_tile_lists(jax.random.fold_in(jax.random.fold_in(key_list[4], part), 71), part)
    return {"queries": queries, "keys": keys, "values": values, "tile_lists": tile_lists}


def reference(queries, keys, values, tile_lists):
    row_width = HEADS * HD
    key_tiles = keys.reshape(NTILES, TILE, HEADS, HD)
    value_tiles = values.reshape(NTILES, TILE, HEADS, HD)
    query_tiles = queries.reshape(NTILES, TILE, HEADS, HD)
    score_scale = HD ** -0.5

    def attend(args):
        query_tile, row_lists = args
        picked = row_lists.astype(jnp.int32)
        chosen = key_tiles[picked].reshape(TOPK * TILE, HEADS, HD)
        chosen_values = value_tiles[picked].reshape(TOPK * TILE, HEADS, HD)
        scores = jnp.einsum("qhd,khd->hqk", query_tile.astype(jnp.float32), chosen.astype(jnp.float32),
                            precision=lax.Precision.HIGHEST) * score_scale
        row_top = jnp.max(scores, axis=2, keepdims=True)
        weights = jnp.exp(scores - row_top)
        row_total = jnp.sum(weights, axis=2)
        rounded = lax.optimization_barrier(weights.astype(jnp.bfloat16)).astype(jnp.float32)
        mixture = jnp.einsum("hqk,khd->qhd", rounded, chosen_values.astype(jnp.float32),
                             precision=lax.Precision.HIGHEST)
        mixture = mixture / jnp.transpose(row_total)[:, :, None]
        return mixture.astype(jnp.bfloat16).reshape(TILE, row_width)

    result = lax.map(attend, (query_tiles, tile_lists))
    return result.reshape(NTILES * TILE, row_width)
```

```python
import functools
import math

import jax
import jax.numpy as jnp
from jax import lax
from jax.experimental import pallas as pl
from jax.experimental.pallas import tpu as pltpu
from jax.sharding import Mesh, PartitionSpec as P

HD = 128
TILE = 64


def score_tile(key_flat, score_scale, query_tile, row_index):
    gathered = key_flat[row_index]
    scores = (
        jnp.einsum("qhd,khtd->hqkt", query_tile, gathered, preferred_element_type=jnp.float32)
        * score_scale
    )
    row_top = jnp.max(scores, axis=(2, 3), keepdims=True)
    weights = jnp.exp(scores - row_top)
    row_total = jnp.sum(weights, axis=(2, 3))
    return (weights.astype(jnp.bfloat16), row_total)


def mix_tile(value_flat, rounded, row_total, row_index):
    gathered = value_flat[row_index]
    mixture = jnp.einsum("hqkt,khtd->qhd", rounded, gathered, preferred_element_type=jnp.float32)
    mixture = mixture / jnp.transpose(row_total)[:, :, None]
    return mixture.astype(jnp.bfloat16).reshape(mixture.shape[0], -1)


def select_slots(
    pick_table, arrays, seq_count, capacity, shard_tiles, tile_rows, local_heads, head_dim
):
    count = len(arrays)
    stacked = jnp.stack(arrays, 0).reshape(count, shard_tiles, tile_rows, local_heads, head_dim)
    stacked = stacked.transpose(1, 0, 3, 2, 4).reshape(shard_tiles, -1)
    outgoing = jnp.dot(pick_table, stacked, preferred_element_type=jnp.float32).astype(jnp.bfloat16)
    return outgoing.reshape(seq_count, capacity, count, local_heads, tile_rows, head_dim)


def slot_plan(queries, keys, values, tile_lists):
    seq_count = lax.axis_size("seq")
    head_count = lax.axis_size("head")
    head_dim = HD
    tile_rows = TILE
    total_tiles, top_count = tile_lists.shape
    local_heads = queries.shape[1] // head_dim // head_count
    local_rows = queries.shape[0] * head_count
    shard_tiles = local_rows // tile_rows
    capacity = 64 // seq_count
    seq_index = lax.axis_index("seq")
    score_scale = head_dim ** (-0.5)
    tile_ids = seq_index * shard_tiles + jnp.arange(shard_tiles, dtype=jnp.int32)
    by_run = tile_lists.reshape(seq_count, shard_tiles * top_count)
    need_out = jnp.any(by_run[:, :, None] == tile_ids[None, None, :], axis=1)
    slot_out = jnp.cumsum(need_out.astype(jnp.int32), axis=1) - 1
    slot_ids = jnp.arange(capacity, dtype=jnp.int32)
    pick_table = need_out[:, None, :] & (slot_out[:, None, :] == slot_ids[None, :, None])
    pick_table = pick_table.astype(jnp.bfloat16).reshape(seq_count * capacity, shard_tiles)
    own_lists = lax.dynamic_slice_in_dim(tile_lists, seq_index * shard_tiles, shard_tiles, 0)
    all_ids = jnp.arange(total_tiles, dtype=jnp.int32)
    matches = own_lists[:, :, None] == all_ids[None, None, :]
    listed = jnp.any(matches, axis=1).reshape(shard_tiles, seq_count, shard_tiles)
    need_in = jnp.any(listed, axis=0)
    slot_in = jnp.cumsum(need_in.astype(jnp.int32), axis=1) - 1
    queries_local, keys_local, values_local = (
        lax.all_to_all(queries, "head", split_axis=1, concat_axis=0, tiled=True),
        lax.all_to_all(keys, "head", split_axis=1, concat_axis=0, tiled=True),
        lax.all_to_all(values, "head", split_axis=1, concat_axis=0, tiled=True),
    )
    received = lax.all_to_all(
        select_slots(
            pick_table,
            (keys_local, values_local),
            seq_count,
            capacity,
            shard_tiles,
            tile_rows,
            local_heads,
            head_dim,
        ),
        "seq",
        split_axis=0,
        concat_axis=0,
        tiled=True,
    )
    key_slots = received[:, :, 0]
    value_slots = received[:, :, 1]
    flat_slots = jnp.broadcast_to(slot_in.reshape(1, 1, total_tiles), matches.shape)
    listed_slot = jnp.sum(jnp.where(matches, flat_slots, 0), axis=2)
    source_run = own_lists // shard_tiles
    slot_index = source_run * capacity + listed_slot
    query_tiles = queries_local.reshape(shard_tiles, tile_rows, local_heads, head_dim)
    slot_shape = (seq_count * capacity, local_heads, tile_rows, head_dim)
    key_flat = key_slots.reshape(slot_shape)
    value_flat = value_slots.reshape(slot_shape)

    def joined_tile(args):
        rounded, row_total = score_tile(key_flat, score_scale, args[0], args[1])
        return mix_tile(value_flat, rounded, row_total, args[1])

    attended = lax.map(joined_tile, (query_tiles, slot_index))
    attended = attended.reshape(local_rows, local_heads * head_dim)
    return lax.all_to_all(attended, "head", split_axis=0, concat_axis=1, tiled=True)


PLANES = 4
SIDE = 2
AXES = ("groups", "z", "y", "head")
SWAP = [(0, 1), (1, 0), (2, 3), (3, 2)]
INWARD = [(0, 1), (3, 2)]
OUTWARD = [(1, 0), (2, 3)]
CROSS = [(1, 2), (2, 1)]
EXPONENT = HD**-0.5 * math.log2(math.e)
UNROLL = 4


def attend_kernel(count, lists, *refs, top_count, sources, slots):
    ends, queries = refs[0], refs[1 : 1 + sources]
    picks = refs[1 + sources : 1 + sources + 2 * slots]
    out, query_buf, key_buf, value_buf, sems = refs[1 + sources + 2 * slots :]
    tiles = key_buf.shape[0] // PLANES
    own = queries[0].shape[0]
    at_end = ends[0] == 1

    def move(src, dst, sem):
        return pltpu.make_async_copy(src, dst, sem)

    def part(buf, slot):
        return buf.at[pl.ds(slot * tiles, tiles)]

    @pl.when(count[0] > 0)
    def _():
        for at, ref in enumerate(queries):
            move(ref, query_buf.at[pl.ds(at * own, own)], sems.at[0]).start()
        for kind, buf in enumerate((key_buf, value_buf)):
            given = picks[kind * slots : (kind + 1) * slots]
            for slot in range(2):
                move(given[slot], part(buf, slot), sems.at[1 + kind]).start()
            if slots == PLANES:
                for slot in range(2, PLANES):
                    move(given[slot], part(buf, slot), sems.at[1 + kind]).start()
            else:

                @pl.when(at_end)
                def _():
                    for slot in range(2, PLANES):
                        move(given[slot + 2], part(buf, slot), sems.at[1 + kind]).start()

                @pl.when(jnp.logical_not(at_end))
                def _():
                    for slot in range(2, PLANES):
                        move(given[slot], part(buf, slot), sems.at[1 + kind]).start()

        move(query_buf, query_buf, sems.at[0]).wait()
        move(key_buf, key_buf, sems.at[1]).wait()
        move(value_buf, value_buf, sems.at[2]).wait()

    def one(row):
        keys = jnp.concatenate([key_buf[lists[row, t]] for t in range(top_count)], axis=0)
        scores = lax.dot_general(
            query_buf[row], keys, (((1,), (1,)), ((), ())), preferred_element_type=jnp.float32
        )
        row_top = jnp.max(scores, axis=1, keepdims=True)
        weights = jnp.exp2((scores - row_top) * EXPONENT)
        row_total = jnp.sum(weights, axis=1, keepdims=True)
        values = jnp.concatenate([value_buf[lists[row, t]] for t in range(top_count)], axis=0)
        mixture = jnp.dot(weights.astype(jnp.bfloat16), values, preferred_element_type=jnp.float32)
        out[row] = (mixture / row_total).astype(jnp.bfloat16)

    def step(at, carry):
        for sub in range(UNROLL):
            one(at * UNROLL + sub)
        return carry

    lax.fori_loop(0, count[0] // UNROLL, step, 0)


def attend(count, lists, ends, queries, keys, values):
    sources, slots = len(queries), len(keys)
    tiles = queries[0].shape[0]
    top_count = lists.shape[1]
    rows = sources * tiles
    kernel = functools.partial(attend_kernel, top_count=top_count, sources=sources, slots=slots)
    work = 4 * rows * TILE * top_count * TILE * HD
    return pl.pallas_call(
        kernel,
        out_shape=jax.ShapeDtypeStruct((rows, TILE, HD), jnp.bfloat16),
        in_specs=[pl.BlockSpec(memory_space=pltpu.SMEM)] * 3
        + [pl.BlockSpec(memory_space=pl.ANY)] * (sources + 2 * slots),
        out_specs=pl.BlockSpec(memory_space=pltpu.VMEM),
        scratch_shapes=[
            pltpu.VMEM((rows, TILE, HD), jnp.bfloat16),
            pltpu.VMEM((PLANES * tiles, TILE, HD), jnp.bfloat16),
            pltpu.VMEM((PLANES * tiles, TILE, HD), jnp.bfloat16),
            pltpu.SemaphoreType.DMA((3,)),
        ],
        compiler_params=pltpu.CompilerParams(vmem_limit_bytes=40 * 1024 * 1024),
        cost_estimate=pl.CostEstimate(
            flops=work * 8, bytes_accessed=2 * PLANES * tiles * TILE * HD * 2, transcendentals=0
        ),
    )(count, lists, ends, *queries, *keys, *values)


def relay_plan(queries, keys, values, tile_lists):
    z = lax.axis_index("z")
    lanes = SIDE * lax.axis_size("head")
    width = lanes * HD
    chunks = queries.shape[1] // width
    plane_tiles = tile_lists.shape[0] // PLANES
    at_end = (z == 0) | (z == PLANES - 1)

    def spread(arrays, chunk):
        cut = [a[:, chunk * width : (chunk + 1) * width] for a in arrays]
        if len(cut) == 1:
            got = lax.all_to_all(cut[0], ("y", "head"), split_axis=1, concat_axis=0, tiled=True)
            return [got.reshape(plane_tiles, TILE, HD)]
        both = jnp.stack(cut)
        got = lax.all_to_all(both, ("y", "head"), split_axis=2, concat_axis=1, tiled=True)
        return [got[i].reshape(plane_tiles, TILE, HD) for i in range(len(cut))]

    def send(array, pairs):
        return lax.ppermute(array, "z", pairs)

    far = z >= PLANES // 2
    rows = jnp.stack(
        [
            lax.dynamic_slice_in_dim(tile_lists, z * plane_tiles, plane_tiles, 0),
            lax.dynamic_slice_in_dim(tile_lists, (z ^ 1) * plane_tiles, plane_tiles, 0),
        ]
    ).reshape(2 * plane_tiles, -1)
    plane = rows // plane_tiles
    plane = jnp.where(far, PLANES - 1 - plane, plane)
    near = jnp.where(far, PLANES - 1 - z, z)
    slot = jnp.where(plane < 2, plane ^ near, plane)
    lists = slot * plane_tiles + rows % plane_tiles
    ends = at_end.astype(jnp.int32).reshape(1)
    inner_count = jnp.where(at_end, 0, 2 * plane_tiles).astype(jnp.int32).reshape(1)
    own_count = jnp.full((1,), plane_tiles, jnp.int32)

    done = []
    for chunk in range(chunks):
        last = chunk == chunks - 1
        if chunk == 0:
            (own_k,) = spread([keys], chunk)
            own_v, own_q = spread([values, queries], chunk)
        else:
            own_k, own_v, own_q = spread([keys, values, queries], chunk)
        held = []
        for own in (own_k, own_v):
            beside = send(own, SWAP if last else INWARD)
            across = send(own, CROSS)
            beyond = send(beside, CROSS)
            got = [own, beside, across, beyond]
            if last:
                got += [send(across, OUTWARD), send(beyond, OUTWARD)]
            held.append(got)
        if last:
            mixed = attend(own_count, lists[:plane_tiles], ends, [own_q], held[0], held[1])
        else:
            near_q = send(own_q, INWARD)
            both = attend(inner_count, lists, ends, [own_q, near_q], held[0], held[1])
            back = send(both[plane_tiles:], OUTWARD)
            mixed = jnp.where(at_end, back, both[:plane_tiles])
        mixed = mixed.reshape(plane_tiles * TILE, HD)
        done.append(lax.all_to_all(mixed, ("y", "head"), split_axis=0, concat_axis=1, tiled=True))
    return jnp.concatenate(done, axis=1)


def solution(mesh):
    seq_count, head_count = mesh.shape["seq"], mesh.shape["head"]
    if seq_count == PLANES * SIDE:
        planned = Mesh(mesh.devices.reshape(-1, PLANES, SIDE, head_count), AXES)
        plan, tokens = relay_plan, AXES
    else:
        planned, plan, tokens = mesh, slot_plan, ("groups", "seq", "head")
    placed = P(tokens, None)
    return jax.shard_map(
        plan,
        mesh=planned,
        in_specs=(placed, placed, placed, P("groups", None)),
        out_specs=placed,
        check_vma=False,
    )
```

```python
import functools
import math

import jax
import jax.numpy as jnp
from jax import lax
from jax.experimental import pallas as pl
from jax.experimental.pallas import tpu as pltpu
from jax.sharding import Mesh, PartitionSpec as P

HD = 128
TILE = 64


def score_tile(key_flat, score_scale, query_tile, row_index):
    gathered = key_flat[row_index]
    scores = (
        jnp.einsum("qhd,khtd->hqkt", query_tile, gathered, preferred_element_type=jnp.float32)
        * score_scale
    )
    row_top = jnp.max(scores, axis=(2, 3), keepdims=True)
    weights = jnp.exp(scores - row_top)
    row_total = jnp.sum(weights, axis=(2, 3))
    return (weights.astype(jnp.bfloat16), row_total)


def mix_tile(value_flat, rounded, row_total, row_index):
    gathered = value_flat[row_index]
    mixture = jnp.einsum("hqkt,khtd->qhd", rounded, gathered, preferred_element_type=jnp.float32)
    mixture = mixture / jnp.transpose(row_total)[:, :, None]
    return mixture.astype(jnp.bfloat16).reshape(mixture.shape[0], -1)


def select_slots(
    pick_table, arrays, seq_count, capacity, shard_tiles, tile_rows, local_heads, head_dim
):
    count = len(arrays)
    stacked = jnp.stack(arrays, 0).reshape(count, shard_tiles, tile_rows, local_heads, head_dim)
    stacked = stacked.transpose(1, 0, 3, 2, 4).reshape(shard_tiles, -1)
    outgoing = jnp.dot(pick_table, stacked, preferred_element_type=jnp.float32).astype(jnp.bfloat16)
    return outgoing.reshape(seq_count, capacity, count, local_heads, tile_rows, head_dim)


def slot_plan(queries, keys, values, tile_lists):
    seq_count = lax.axis_size("seq")
    head_count = lax.axis_size("head")
    head_dim = HD
    tile_rows = TILE
    total_tiles, top_count = tile_lists.shape
    local_heads = queries.shape[1] // head_dim // head_count
    local_rows = queries.shape[0] * head_count
    shard_tiles = local_rows // tile_rows
    capacity = 64 // seq_count
    seq_index = lax.axis_index("seq")
    score_scale = head_dim ** (-0.5)
    tile_ids = seq_index * shard_tiles + jnp.arange(shard_tiles, dtype=jnp.int32)
    by_run = tile_lists.reshape(seq_count, shard_tiles * top_count)
    need_out = jnp.any(by_run[:, :, None] == tile_ids[None, None, :], axis=1)
    slot_out = jnp.cumsum(need_out.astype(jnp.int32), axis=1) - 1
    slot_ids = jnp.arange(capacity, dtype=jnp.int32)
    pick_table = need_out[:, None, :] & (slot_out[:, None, :] == slot_ids[None, :, None])
    pick_table = pick_table.astype(jnp.bfloat16).reshape(seq_count * capacity, shard_tiles)
    own_lists = lax.dynamic_slice_in_dim(tile_lists, seq_index * shard_tiles, shard_tiles, 0)
    all_ids = jnp.arange(total_tiles, dtype=jnp.int32)
    matches = own_lists[:, :, None] == all_ids[None, None, :]
    listed = jnp.any(matches, axis=1).reshape(shard_tiles, seq_count, shard_tiles)
    need_in = jnp.any(listed, axis=0)
    slot_in = jnp.cumsum(need_in.astype(jnp.int32), axis=1) - 1
    queries_local, keys_local, values_local = (
        lax.all_to_all(queries, "head", split_axis=1, concat_axis=0, tiled=True),
        lax.all_to_all(keys, "head", split_axis=1, concat_axis=0, tiled=True),
        lax.all_to_all(values, "head", split_axis=1, concat_axis=0, tiled=True),
    )
    received = lax.all_to_all(
        select_slots(
            pick_table,
            (keys_local, values_local),
            seq_count,
            capacity,
            shard_tiles,
            tile_rows,
            local_heads,
            head_dim,
        ),
        "seq",
        split_axis=0,
        concat_axis=0,
        tiled=True,
    )
    key_slots = received[:, :, 0]
    value_slots = received[:, :, 1]
    flat_slots = jnp.broadcast_to(slot_in.reshape(1, 1, total_tiles), matches.shape)
    listed_slot = jnp.sum(jnp.where(matches, flat_slots, 0), axis=2)
    source_run = own_lists // shard_tiles
    slot_index = source_run * capacity + listed_slot
    query_tiles = queries_local.reshape(shard_tiles, tile_rows, local_heads, head_dim)
    slot_shape = (seq_count * capacity, local_heads, tile_rows, head_dim)
    key_flat = key_slots.reshape(slot_shape)
    value_flat = value_slots.reshape(slot_shape)

    def joined_tile(args):
        rounded, row_total = score_tile(key_flat, score_scale, args[0], args[1])
        return mix_tile(value_flat, rounded, row_total, args[1])

    attended = lax.map(joined_tile, (query_tiles, slot_index))
    attended = attended.reshape(local_rows, local_heads * head_dim)
    return lax.all_to_all(attended, "head", split_axis=0, concat_axis=1, tiled=True)


PLANES = 4
SIDE = 2
AXES = ("groups", "z", "y", "head")
RANKS = ("y", "head")
INWARD = [(0, 1), (3, 2)]
OUTWARD = [(1, 0), (2, 3)]
CROSS = [(1, 2), (2, 1)]
EXPONENT = HD**-0.5 * math.log2(math.e)
UNROLL = 4
COST = 11 * 10**9
VMEM_LIMIT = 60 * 1024 * 1024


def shuffle_kernel(*refs, parts, source_count):
    sources, outs = refs[:source_count], refs[source_count : source_count + len(parts)]
    bufs, sems = refs[source_count + len(parts) : -1], refs[-1]
    loads, stores = {}, []
    for wanted in parts:
        for which, chunk in wanted:
            width = outs[0].shape[0] * HD
            columns = pl.ds(chunk * width, width)
            loads[which, chunk] = pltpu.make_async_copy(
                sources[which].at[:, columns], bufs[which].at[:, columns], sems.at[len(loads)]
            )
            loads[which, chunk].start()
    for out, wanted in zip(outs, parts):
        for at, (which, chunk) in enumerate(wanted):
            loads[which, chunk].wait()
            for lane in range(out.shape[0]):
                column = (chunk * out.shape[0] + lane) * HD
                store = pltpu.make_async_copy(
                    bufs[which].at[:, pl.ds(column, HD)],
                    out.at[lane, at],
                    sems.at[len(loads) + len(stores)],
                )
                store.start()
                stores.append(store)
    for store in stores:
        store.wait()


def shuffle(arrays, lanes, parts, name):
    rows = arrays[0].shape[0]
    kernel = functools.partial(shuffle_kernel, parts=parts, source_count=len(arrays))
    moved = sum(len(p) for p in parts)
    return pl.pallas_call(
        kernel,
        out_shape=[
            jax.ShapeDtypeStruct((lanes, len(p), rows, HD), arrays[0].dtype) for p in parts
        ],
        in_specs=[pl.BlockSpec(memory_space=pl.ANY)] * len(arrays),
        out_specs=[pl.BlockSpec(memory_space=pl.ANY)] * len(parts),
        scratch_shapes=[pltpu.VMEM(a.shape, a.dtype) for a in arrays]
        + [pltpu.SemaphoreType.DMA((moved * (lanes + 1),))],
        compiler_params=pltpu.CompilerParams(vmem_limit_bytes=VMEM_LIMIT),
        cost_estimate=pl.CostEstimate(
            flops=0, bytes_accessed=2 * moved * lanes * rows * HD * 2, transcendentals=0
        ),
        name=name,
    )(*arrays)


def gather_kernel(*refs):
    sources, out, buf, sems = refs[:-3], refs[-3], refs[-2], refs[-1]
    loads = []
    for source in sources:
        for at in range(source.shape[1]):
            for lane in range(source.shape[0]):
                column = pl.ds(len(loads) * HD, HD)
                load = pltpu.make_async_copy(
                    source.at[lane, at], buf.at[:, column], sems.at[len(loads)]
                )
                load.start()
                loads.append(load)
    for load in loads:
        load.wait()
    store = pltpu.make_async_copy(buf, out, sems.at[len(loads)])
    store.start()
    store.wait()


def gather_out(parts):
    rows = parts[0].shape[2]
    blocks = sum(p.shape[0] * p.shape[1] for p in parts)
    return pl.pallas_call(
        gather_kernel,
        out_shape=jax.ShapeDtypeStruct((rows, blocks * HD), parts[0].dtype),
        in_specs=[pl.BlockSpec(memory_space=pl.ANY)] * len(parts),
        out_specs=pl.BlockSpec(memory_space=pl.ANY),
        scratch_shapes=[
            pltpu.VMEM((rows, blocks * HD), parts[0].dtype),
            pltpu.SemaphoreType.DMA((blocks + 1,)),
        ],
        compiler_params=pltpu.CompilerParams(vmem_limit_bytes=VMEM_LIMIT),
        name="gather_out",
    )(*parts)


def attend_kernel(count, lists, query, *refs, chunk, ats):
    picks = refs[: 2 * PLANES]
    out, query_buf, key_buf, value_buf, score_buf, sems = refs[2 * PLANES :]
    lanes, _, shard_tiles = query.shape[:3]
    tiles = lanes * shard_tiles
    top_count = lists.shape[1]
    blank = jnp.zeros((TILE, HD), jnp.bfloat16)

    def beside(left, right):
        return jnp.concatenate([left, right], axis=1)

    @pl.when(count[0] > 0)
    def _():
        for lane in range(lanes):
            place = pl.ds(lane * shard_tiles, shard_tiles)
            pltpu.make_async_copy(query.at[lane, chunk], query_buf.at[place], sems.at[0]).start()
        for kind, buf in enumerate((key_buf, value_buf)):
            for slot in range(PLANES):
                source, at = picks[kind * PLANES + slot], ats[kind]
                for lane in range(lanes):
                    place = pl.ds((slot * lanes + lane) * shard_tiles, shard_tiles)
                    pltpu.make_async_copy(
                        source.at[lane, at], buf.at[place], sems.at[1 + kind]
                    ).start()
        pltpu.make_async_copy(query_buf, query_buf, sems.at[0]).wait()
        pltpu.make_async_copy(key_buf, key_buf, sems.at[1]).wait()

        def listed(buf, pair, t):
            return beside(buf[lists[2 * pair, t]], buf[lists[2 * pair + 1, t]])

        def score(pair, at):
            wide = jnp.concatenate(
                [beside(query_buf[2 * pair], blank), beside(blank, query_buf[2 * pair + 1])], axis=0
            )
            keys = jnp.concatenate([listed(key_buf, pair, t) for t in range(top_count)], axis=0)
            score_buf[at] = lax.dot_general(
                wide, keys, (((1,), (1,)), ((), ())), preferred_element_type=jnp.float32
            )

        def mix(pair, at):
            scores = score_buf[at]
            row_top = jnp.max(scores, axis=1, keepdims=True)
            weights = jnp.exp2((scores - row_top) * EXPONENT)
            row_total = jnp.sum(weights, axis=1, keepdims=True)
            values = jnp.concatenate([listed(value_buf, pair, t) for t in range(top_count)], axis=0)
            mixture = jnp.dot(
                weights.astype(jnp.bfloat16), values, preferred_element_type=jnp.float32
            )
            first = mixture[:TILE, :HD] / row_total[:TILE]
            second = mixture[TILE:, HD:] / row_total[TILE:]
            out[2 * pair] = first.astype(jnp.bfloat16)
            out[2 * pair + 1] = second.astype(jnp.bfloat16)

        score(0, 0)
        pltpu.make_async_copy(value_buf, value_buf, sems.at[2]).wait()

        def step(at, carry):
            for sub in range(UNROLL):
                pair = at * UNROLL + sub
                score(jnp.minimum(pair + 1, tiles // 2 - 1), (sub + 1) % 2)
                mix(pair, sub % 2)
            return carry

        lax.fori_loop(0, tiles // 2 // UNROLL, step, 0)


def attend(count, lists, query, keys, values, ats, chunk, name):
    tiles, top_count = lists.shape
    lanes = query.shape[0]
    shaped = (lanes, -1, tiles // lanes, TILE, HD)
    return pl.pallas_call(
        functools.partial(attend_kernel, chunk=chunk, ats=ats),
        out_shape=jax.ShapeDtypeStruct((tiles, TILE, HD), jnp.bfloat16),
        in_specs=[pl.BlockSpec(memory_space=pltpu.SMEM)] * 2
        + [pl.BlockSpec(memory_space=pl.ANY)] * (1 + 2 * PLANES),
        out_specs=pl.BlockSpec(memory_space=pltpu.VMEM),
        scratch_shapes=[
            pltpu.VMEM((tiles, TILE, HD), jnp.bfloat16),
            pltpu.VMEM((PLANES * tiles, TILE, HD), jnp.bfloat16),
            pltpu.VMEM((PLANES * tiles, TILE, HD), jnp.bfloat16),
            pltpu.VMEM((2, 2 * TILE, top_count * TILE), jnp.float32),
            pltpu.SemaphoreType.DMA((3,)),
        ],
        compiler_params=pltpu.CompilerParams(vmem_limit_bytes=VMEM_LIMIT),
        cost_estimate=pl.CostEstimate(flops=COST, bytes_accessed=1, transcendentals=0),
        name=name,
    )(count, lists, query.reshape(shaped), *[a.reshape(shaped) for a in (*keys, *values)])


def after(array, *others):
    return lax.optimization_barrier((array, *others))[0]


def relay_plan(queries, keys, values, tile_lists):
    z = lax.axis_index("z")
    lanes = SIDE * lax.axis_size("head")
    chunks = queries.shape[1] // (lanes * HD)
    plane_tiles = tile_lists.shape[0] // PLANES
    at_end = (z == 0) | (z == PLANES - 1)

    def swap(array):
        return lax.all_to_all(array, RANKS, split_axis=0, concat_axis=0, tiled=True)

    def send(array, pairs, name):
        with jax.named_scope(name):
            return lax.ppermute(array, "z", pairs)

    far = z >= PLANES // 2
    rows = jnp.stack(
        [
            lax.dynamic_slice_in_dim(tile_lists, z * plane_tiles, plane_tiles, 0),
            lax.dynamic_slice_in_dim(tile_lists, (z ^ 1) * plane_tiles, plane_tiles, 0),
        ]
    )
    plane = rows // plane_tiles
    plane = jnp.where(far, PLANES - 1 - plane, plane)
    near = jnp.where(far, PLANES - 1 - z, z)
    slot = jnp.where(plane < 2, plane ^ near, plane)
    lists = slot * plane_tiles + rows % plane_tiles
    count = jnp.where(at_end, 0, 1).astype(jnp.int32).reshape(1)

    (first,) = shuffle([keys, values], lanes, [[(0, 0), (1, 0)]], "shuffle_first")
    own_0 = swap(first)
    rest = shuffle(
        [queries, keys, values],
        lanes,
        [[(0, c) for c in range(chunks)]] + [[(1, c), (2, c)] for c in range(1, chunks)],
        "shuffle_rest",
    )
    in_0 = send(own_0, INWARD, "in_0")
    cross_0 = send(own_0, CROSS, "cross_0")
    own_1 = swap(after(rest[1], own_0))
    relay_0 = send(in_0, CROSS, "relay_0")
    in_1 = send(after(own_1, in_0), INWARD, "in_1")
    cross_1 = send(after(own_1, cross_0), CROSS, "cross_1")
    asked = swap(after(rest[0], own_1, cross_0, in_0))
    own_2 = swap(after(rest[2], asked, in_1))
    in_q = send(after(asked, in_1), INWARD, "in_q")
    in_2 = send(after(own_2, in_1), INWARD, "in_2")
    cross_2 = send(after(own_2, relay_0), CROSS, "cross_2")
    relay_1 = send(after(in_1, relay_0), CROSS, "relay_1")

    done = []

    def one(at, chunk, query, pairs):
        return attend(count, lists[at], query, pairs, pairs, (0, 1), chunk, f"attend_{chunk}{at}")

    def home(beside, chunk):
        return send(beside, OUTWARD, f"out_{chunk}")

    def finish(parts):
        mixed = []
        for own, home in parts:
            mixed.append(jnp.where(at_end, home, own).reshape(lanes, -1, HD))
        return mixed[0][:, None] if len(mixed) == 1 else jnp.stack(mixed, axis=1)

    pairs = [own_0, in_0, cross_0, relay_0]
    mine_0 = one(0, 0, after(asked, cross_1, own_2), pairs)
    theirs_0 = one(1, 0, after(in_q, mine_0), pairs)
    relay_2 = send(after(in_2, cross_1, relay_1), CROSS, "relay_2")
    pairs = [own_1, in_1, cross_1, relay_1]
    mine_1 = one(0, 1, after(asked, theirs_0, in_2), pairs)
    theirs_1 = one(1, 1, after(in_q, mine_1), pairs)
    home_0, home_1 = home(theirs_0, 0), home(theirs_1, 1)
    pairs = [own_2, in_2, cross_2, relay_2]
    theirs_2 = one(1, 2, after(in_q, theirs_1), pairs)
    mine_2 = one(0, 2, after(asked, theirs_2), pairs)
    early = swap(finish([(mine_0, after(home_0, theirs_2)), (mine_1, after(home_1, theirs_2))]))
    late = swap(after(finish([(mine_2, home(theirs_2, 2))]), early))
    return gather_out([early, late])


def solution(mesh):
    seq_count, head_count = mesh.shape["seq"], mesh.shape["head"]
    if seq_count == PLANES * SIDE:
        planned = Mesh(mesh.devices.reshape(-1, PLANES, SIDE, head_count), AXES)
        plan, tokens = relay_plan, AXES
    else:
        planned, plan, tokens = mesh, slot_plan, ("groups", "seq", "head")
    placed = P(tokens, None)
    return jax.shard_map(
        plan,
        mesh=planned,
        in_specs=(placed, placed, placed, P("groups", None)),
        out_specs=placed,
        check_vma=False,
    )
```

```python
import functools
import math

import jax
import jax.numpy as jnp
from jax import lax
from jax.experimental import pallas as pl
from jax.experimental.pallas import tpu as pltpu
from jax.sharding import Mesh, PartitionSpec as P

HD = 128
TILE = 64


def score_tile(key_flat, score_scale, query_tile, row_index):
    gathered = key_flat[row_index]
    scores = (
        jnp.einsum("qhd,khtd->hqkt", query_tile, gathered, preferred_element_type=jnp.float32)
        * score_scale
    )
    row_top = jnp.max(scores, axis=(2, 3), keepdims=True)
    weights = jnp.exp(scores - row_top)
    row_total = jnp.sum(weights, axis=(2, 3))
    return (weights.astype(jnp.bfloat16), row_total)


def mix_tile(value_flat, rounded, row_total, row_index):
    gathered = value_flat[row_index]
    mixture = jnp.einsum("hqkt,khtd->qhd", rounded, gathered, preferred_element_type=jnp.float32)
    mixture = mixture / jnp.transpose(row_total)[:, :, None]
    return mixture.astype(jnp.bfloat16).reshape(mixture.shape[0], -1)


def select_slots(
    pick_table, arrays, seq_count, capacity, shard_tiles, tile_rows, local_heads, head_dim
):
    count = len(arrays)
    stacked = jnp.stack(arrays, 0).reshape(count, shard_tiles, tile_rows, local_heads, head_dim)
    stacked = stacked.transpose(1, 0, 3, 2, 4).reshape(shard_tiles, -1)
    outgoing = jnp.dot(pick_table, stacked, preferred_element_type=jnp.float32).astype(jnp.bfloat16)
    return outgoing.reshape(seq_count, capacity, count, local_heads, tile_rows, head_dim)


def slot_plan(queries, keys, values, tile_lists):
    seq_count = lax.axis_size("seq")
    head_count = lax.axis_size("head")
    head_dim = HD
    tile_rows = TILE
    total_tiles, top_count = tile_lists.shape
    local_heads = queries.shape[1] // head_dim // head_count
    local_rows = queries.shape[0] * head_count
    shard_tiles = local_rows // tile_rows
    capacity = 64 // seq_count
    seq_index = lax.axis_index("seq")
    score_scale = head_dim ** (-0.5)
    tile_ids = seq_index * shard_tiles + jnp.arange(shard_tiles, dtype=jnp.int32)
    by_run = tile_lists.reshape(seq_count, shard_tiles * top_count)
    need_out = jnp.any(by_run[:, :, None] == tile_ids[None, None, :], axis=1)
    slot_out = jnp.cumsum(need_out.astype(jnp.int32), axis=1) - 1
    slot_ids = jnp.arange(capacity, dtype=jnp.int32)
    pick_table = need_out[:, None, :] & (slot_out[:, None, :] == slot_ids[None, :, None])
    pick_table = pick_table.astype(jnp.bfloat16).reshape(seq_count * capacity, shard_tiles)
    own_lists = lax.dynamic_slice_in_dim(tile_lists, seq_index * shard_tiles, shard_tiles, 0)
    all_ids = jnp.arange(total_tiles, dtype=jnp.int32)
    matches = own_lists[:, :, None] == all_ids[None, None, :]
    listed = jnp.any(matches, axis=1).reshape(shard_tiles, seq_count, shard_tiles)
    need_in = jnp.any(listed, axis=0)
    slot_in = jnp.cumsum(need_in.astype(jnp.int32), axis=1) - 1
    queries_local, keys_local, values_local = (
        lax.all_to_all(queries, "head", split_axis=1, concat_axis=0, tiled=True),
        lax.all_to_all(keys, "head", split_axis=1, concat_axis=0, tiled=True),
        lax.all_to_all(values, "head", split_axis=1, concat_axis=0, tiled=True),
    )
    received = lax.all_to_all(
        select_slots(
            pick_table,
            (keys_local, values_local),
            seq_count,
            capacity,
            shard_tiles,
            tile_rows,
            local_heads,
            head_dim,
        ),
        "seq",
        split_axis=0,
        concat_axis=0,
        tiled=True,
    )
    key_slots = received[:, :, 0]
    value_slots = received[:, :, 1]
    flat_slots = jnp.broadcast_to(slot_in.reshape(1, 1, total_tiles), matches.shape)
    listed_slot = jnp.sum(jnp.where(matches, flat_slots, 0), axis=2)
    source_run = own_lists // shard_tiles
    slot_index = source_run * capacity + listed_slot
    query_tiles = queries_local.reshape(shard_tiles, tile_rows, local_heads, head_dim)
    slot_shape = (seq_count * capacity, local_heads, tile_rows, head_dim)
    key_flat = key_slots.reshape(slot_shape)
    value_flat = value_slots.reshape(slot_shape)

    def joined_tile(args):
        rounded, row_total = score_tile(key_flat, score_scale, args[0], args[1])
        return mix_tile(value_flat, rounded, row_total, args[1])

    attended = lax.map(joined_tile, (query_tiles, slot_index))
    attended = attended.reshape(local_rows, local_heads * head_dim)
    return lax.all_to_all(attended, "head", split_axis=0, concat_axis=1, tiled=True)


PLANES = 4
SIDE = 2
AXES = ("groups", "z", "y", "head")
RANKS = ("y", "head")
INWARD = [(0, 1), (3, 2)]
OUTWARD = [(1, 0), (2, 3)]
CROSS = [(1, 2), (2, 1)]
EXPONENT = HD**-0.5 * math.log2(math.e)
COST = 9 * 10**9
LONG = 24 * 10**9
VMEM_LIMIT = 60 * 1024 * 1024


def shuffle_kernel(*refs, parts, source_count):
    sources, outs = refs[:source_count], refs[source_count : source_count + len(parts)]
    bufs, sems = refs[source_count + len(parts) : -1], refs[-1]
    loads, stores = {}, []
    for wanted in parts:
        for which, chunk in wanted:
            width = outs[0].shape[0] * HD
            columns = pl.ds(chunk * width, width)
            loads[which, chunk] = pltpu.make_async_copy(
                sources[which].at[:, columns], bufs[which].at[:, columns], sems.at[len(loads)]
            )
            loads[which, chunk].start()
    for out, wanted in zip(outs, parts):
        for at, (which, chunk) in enumerate(wanted):
            loads[which, chunk].wait()
            for lane in range(out.shape[0]):
                column = (chunk * out.shape[0] + lane) * HD
                store = pltpu.make_async_copy(
                    bufs[which].at[:, pl.ds(column, HD)],
                    out.at[lane, at],
                    sems.at[len(loads) + len(stores)],
                )
                store.start()
                stores.append(store)
    for store in stores:
        store.wait()


def shuffle(arrays, lanes, parts, name):
    rows = arrays[0].shape[0]
    kernel = functools.partial(shuffle_kernel, parts=parts, source_count=len(arrays))
    moved = sum(len(p) for p in parts)
    return pl.pallas_call(
        kernel,
        out_shape=[
            jax.ShapeDtypeStruct((lanes, len(p), rows, HD), arrays[0].dtype) for p in parts
        ],
        in_specs=[pl.BlockSpec(memory_space=pl.ANY)] * len(arrays),
        out_specs=[pl.BlockSpec(memory_space=pl.ANY)] * len(parts),
        scratch_shapes=[pltpu.VMEM(a.shape, a.dtype) for a in arrays]
        + [pltpu.SemaphoreType.DMA((moved * (lanes + 1),))],
        compiler_params=pltpu.CompilerParams(vmem_limit_bytes=VMEM_LIMIT),
        cost_estimate=pl.CostEstimate(
            flops=0, bytes_accessed=2 * moved * lanes * rows * HD * 2, transcendentals=0
        ),
        name=name,
    )(*arrays)


def gather_kernel(*refs):
    sources, out, buf, sems = refs[:-3], refs[-3], refs[-2], refs[-1]
    loads = []
    for source in sources:
        for at in range(source.shape[1]):
            for lane in range(source.shape[0]):
                column = pl.ds(len(loads) * HD, HD)
                load = pltpu.make_async_copy(
                    source.at[lane, at], buf.at[:, column], sems.at[len(loads)]
                )
                load.start()
                loads.append(load)
    for load in loads:
        load.wait()
    store = pltpu.make_async_copy(buf, out, sems.at[len(loads)])
    store.start()
    store.wait()


def gather_out(parts):
    rows = parts[0].shape[2]
    blocks = sum(p.shape[0] * p.shape[1] for p in parts)
    return pl.pallas_call(
        gather_kernel,
        out_shape=jax.ShapeDtypeStruct((rows, blocks * HD), parts[0].dtype),
        in_specs=[pl.BlockSpec(memory_space=pl.ANY)] * len(parts),
        out_specs=pl.BlockSpec(memory_space=pl.ANY),
        scratch_shapes=[
            pltpu.VMEM((rows, blocks * HD), parts[0].dtype),
            pltpu.SemaphoreType.DMA((blocks + 1,)),
        ],
        compiler_params=pltpu.CompilerParams(vmem_limit_bytes=VMEM_LIMIT),
        name="gather_out",
    )(*parts)


def attend_kernel(count, lists, query, *refs, chunk, ats):
    picks = refs[: 2 * PLANES]
    outs = refs[2 * PLANES : -5]
    query_buf, key_buf, value_buf, score_buf, sems = refs[-5:]
    share = outs[0].shape[0]
    lanes, _, shard_tiles = query.shape[:3]
    tiles = lanes * shard_tiles
    top_count = lists.shape[1]
    blank = jnp.zeros((TILE, HD), jnp.bfloat16)

    def beside(left, right):
        return jnp.concatenate([left, right], axis=1)

    @pl.when(count[0] > 0)
    def _():
        for lane in range(lanes):
            place = pl.ds(lane * shard_tiles, shard_tiles)
            pltpu.make_async_copy(query.at[lane, chunk], query_buf.at[place], sems.at[0]).start()
        for kind, buf in enumerate((key_buf, value_buf)):
            for slot in range(PLANES):
                source, at = picks[kind * PLANES + slot], ats[kind]
                for lane in range(lanes):
                    place = pl.ds((slot * lanes + lane) * shard_tiles, shard_tiles)
                    pltpu.make_async_copy(
                        source.at[lane, at], buf.at[place], sems.at[1 + kind]
                    ).start()
        pltpu.make_async_copy(query_buf, query_buf, sems.at[0]).wait()
        pltpu.make_async_copy(key_buf, key_buf, sems.at[1]).wait()

        def listed(buf, pair, t):
            return beside(buf[lists[2 * pair, t]], buf[lists[2 * pair + 1, t]])

        def score(pair, at):
            wide = jnp.concatenate(
                [beside(query_buf[2 * pair], blank), beside(blank, query_buf[2 * pair + 1])], axis=0
            )
            keys = jnp.concatenate([listed(key_buf, pair, t) for t in range(top_count)], axis=0)
            score_buf[at] = lax.dot_general(
                wide, keys, (((1,), (1,)), ((), ())), preferred_element_type=jnp.float32
            )

        def mix(pair, at):
            scores = score_buf[at]
            row_top = jnp.max(scores, axis=1, keepdims=True)
            weights = jnp.exp2((scores - row_top) * EXPONENT)
            row_total = jnp.sum(weights, axis=1, keepdims=True)
            values = jnp.concatenate([listed(value_buf, pair, t) for t in range(top_count)], axis=0)
            mixture = jnp.dot(
                weights.astype(jnp.bfloat16), values, preferred_element_type=jnp.float32
            )
            first = mixture[:TILE, :HD] / row_total[:TILE]
            second = mixture[TILE:, HD:] / row_total[TILE:]
            out, row = outs[2 * pair // share], 2 * pair % share
            out[row] = first.astype(jnp.bfloat16)
            out[row + 1] = second.astype(jnp.bfloat16)

        score(0, 0)
        pltpu.make_async_copy(value_buf, value_buf, sems.at[2]).wait()

        for pair in range(tiles // 2):
            if pair + 1 < tiles // 2:
                score(pair + 1, (pair + 1) % 2)
            mix(pair, pair % 2)


def attend(count, lists, query, keys, values, ats, chunk, cost, name, pieces=1):
    tiles, top_count = lists.shape
    lanes = query.shape[0]
    shaped = (lanes, -1, tiles // lanes, TILE, HD)
    return pl.pallas_call(
        functools.partial(attend_kernel, chunk=chunk, ats=ats),
        out_shape=[jax.ShapeDtypeStruct((tiles // pieces, TILE, HD), jnp.bfloat16)] * pieces,
        in_specs=[pl.BlockSpec(memory_space=pltpu.SMEM)] * 2
        + [pl.BlockSpec(memory_space=pl.ANY)] * (1 + 2 * PLANES),
        out_specs=[pl.BlockSpec(memory_space=pltpu.VMEM)] * pieces,
        scratch_shapes=[
            pltpu.VMEM((tiles, TILE, HD), jnp.bfloat16),
            pltpu.VMEM((PLANES * tiles, TILE, HD), jnp.bfloat16),
            pltpu.VMEM((PLANES * tiles, TILE, HD), jnp.bfloat16),
            pltpu.VMEM((2, 2 * TILE, top_count * TILE), jnp.float32),
            pltpu.SemaphoreType.DMA((3,)),
        ],
        compiler_params=pltpu.CompilerParams(vmem_limit_bytes=VMEM_LIMIT),
        cost_estimate=pl.CostEstimate(flops=cost, bytes_accessed=1, transcendentals=0),
        name=name,
    )(count, lists, query.reshape(shaped), *[a.reshape(shaped) for a in (*keys, *values)])


def after(array, *others):
    return lax.optimization_barrier((array, *others))[0]


def relay_plan(queries, keys, values, tile_lists):
    z = lax.axis_index("z")
    lanes = SIDE * lax.axis_size("head")
    chunks = queries.shape[1] // (lanes * HD)
    plane_tiles = tile_lists.shape[0] // PLANES
    at_end = (z == 0) | (z == PLANES - 1)

    def swap(array):
        return lax.all_to_all(array, RANKS, split_axis=0, concat_axis=0, tiled=True)

    def send(array, pairs, name):
        with jax.named_scope(name):
            return lax.ppermute(array, "z", pairs)

    far = z >= PLANES // 2
    rows = jnp.stack(
        [
            lax.dynamic_slice_in_dim(tile_lists, z * plane_tiles, plane_tiles, 0),
            lax.dynamic_slice_in_dim(tile_lists, (z ^ 1) * plane_tiles, plane_tiles, 0),
        ]
    )
    plane = rows // plane_tiles
    plane = jnp.where(far, PLANES - 1 - plane, plane)
    near = jnp.where(far, PLANES - 1 - z, z)
    slot = jnp.where(plane < 2, plane ^ near, plane)
    lists = slot * plane_tiles + rows % plane_tiles
    count = jnp.where(at_end, 0, 1).astype(jnp.int32).reshape(1)

    (first,) = shuffle([keys, values], lanes, [[(0, 0), (1, 0)]], "shuffle_first")
    own_0 = swap(first)
    rest_1, rest_q0, rest_2, rest_q = shuffle(
        [queries, keys, values],
        lanes,
        [[(1, 1), (2, 1)], [(0, 0), (0, 1)], [(1, 2), (2, 2)], [(0, 2)]],
        "shuffle_rest",
    )
    in_0 = send(own_0, INWARD, "in_0")
    cross_0 = send(own_0, CROSS, "cross_0")
    own_1 = swap(after(rest_1, own_0))
    relay_0 = send(after(in_0, cross_0), CROSS, "relay_0")
    in_1 = send(after(own_1, in_0), INWARD, "in_1")
    cross_1 = send(after(own_1, cross_0), CROSS, "cross_1")
    asked_0 = swap(after(rest_q0, own_1, cross_0, in_0))
    in_q0 = send(after(asked_0, in_0), INWARD, "in_q0")
    own_2 = swap(after(rest_2, asked_0))
    relay_1 = send(after(in_1, relay_0), CROSS, "relay_1")
    in_2 = send(after(own_2, in_1), INWARD, "in_2")
    cross_2 = send(after(own_2, relay_0, cross_1), CROSS, "cross_2")
    asked = swap(after(rest_q, own_2))
    in_q = send(after(asked, in_q0), INWARD, "in_q")
    relay_2 = send(after(in_2, relay_1), CROSS, "relay_2")

    def one(at, chunk, query, pairs, place, cost=COST, pieces=1):
        name = f"attend_{chunk}{at}"
        got = attend(count, lists[at], query, pairs, pairs, (0, 1), place, cost, name, pieces)
        return got if pieces > 1 else got[0]

    def home(beside, chunk):
        return send(beside, OUTWARD, f"out_{chunk}")

    def finish(parts):
        mixed = []
        for own, home in parts:
            mixed.append(jnp.where(at_end, home, own).reshape(lanes, -1, HD))
        return mixed[0][:, None] if len(mixed) == 1 else jnp.stack(mixed, axis=1)

    pairs = [own_0, in_0, cross_0, relay_0]
    mine_0 = one(0, 0, asked_0, pairs, 0)
    theirs_0 = one(1, 0, after(in_q0, mine_0), pairs, 0)
    home_0 = home(theirs_0, 0)
    pairs = [own_1, in_1, cross_1, relay_1]
    mine_1 = one(0, 1, after(asked_0, theirs_0), pairs, 1)
    theirs_1 = one(1, 1, after(in_q0, mine_1), pairs, 1, LONG)
    home_1 = home(theirs_1, 1)
    mixed = finish([(mine_0, home_0), (mine_1, home_1)])
    early = swap(mixed)
    pairs = [own_2, in_2, cross_2, relay_2]
    theirs_2 = one(1, 2, after(in_q, theirs_1, mixed), pairs, 0, 1)
    mine_2 = one(0, 2, after(asked, theirs_2), pairs, 0, 1)
    home_2 = home(theirs_2, 2)
    late = swap(after(finish([(mine_2, home_2)]), early))
    return gather_out([early, late])


def solution(mesh):
    seq_count, head_count = mesh.shape["seq"], mesh.shape["head"]
    if seq_count == PLANES * SIDE:
        planned = Mesh(mesh.devices.reshape(-1, PLANES, SIDE, head_count), AXES)
        plan, tokens = relay_plan, AXES
    else:
        planned, plan, tokens = mesh, slot_plan, ("groups", "seq", "head")
    placed = P(tokens, None)
    return jax.shard_map(
        plan,
        mesh=planned,
        in_specs=(placed, placed, placed, P("groups", None)),
        out_specs=placed,
        check_vma=False,
    )
```

```python
import functools
import math

import jax
import jax.numpy as jnp
from jax import lax
from jax.experimental import pallas as pl
from jax.experimental.pallas import tpu as pltpu
from jax.sharding import Mesh, PartitionSpec as P

HD = 128
TILE = 64


def score_tile(key_flat, score_scale, query_tile, row_index):
    gathered = key_flat[row_index]
    scores = (
        jnp.einsum("qhd,khtd->hqkt", query_tile, gathered, preferred_element_type=jnp.float32)
        * score_scale
    )
    row_top = jnp.max(scores, axis=(2, 3), keepdims=True)
    weights = jnp.exp(scores - row_top)
    row_total = jnp.sum(weights, axis=(2, 3))
    return (weights.astype(jnp.bfloat16), row_total)


def mix_tile(value_flat, rounded, row_total, row_index):
    gathered = value_flat[row_index]
    mixture = jnp.einsum("hqkt,khtd->qhd", rounded, gathered, preferred_element_type=jnp.float32)
    mixture = mixture / jnp.transpose(row_total)[:, :, None]
    return mixture.astype(jnp.bfloat16).reshape(mixture.shape[0], -1)


def select_slots(
    pick_table, arrays, seq_count, capacity, shard_tiles, tile_rows, local_heads, head_dim
):
    count = len(arrays)
    stacked = jnp.stack(arrays, 0).reshape(count, shard_tiles, tile_rows, local_heads, head_dim)
    stacked = stacked.transpose(1, 0, 3, 2, 4).reshape(shard_tiles, -1)
    outgoing = jnp.dot(pick_table, stacked, preferred_element_type=jnp.float32).astype(jnp.bfloat16)
    return outgoing.reshape(seq_count, capacity, count, local_heads, tile_rows, head_dim)


def slot_plan(queries, keys, values, tile_lists):
    seq_count = lax.axis_size("seq")
    head_count = lax.axis_size("head")
    head_dim = HD
    tile_rows = TILE
    total_tiles, top_count = tile_lists.shape
    local_heads = queries.shape[1] // head_dim // head_count
    local_rows = queries.shape[0] * head_count
    shard_tiles = local_rows // tile_rows
    capacity = 64 // seq_count
    seq_index = lax.axis_index("seq")
    score_scale = head_dim ** (-0.5)
    tile_ids = seq_index * shard_tiles + jnp.arange(shard_tiles, dtype=jnp.int32)
    by_run = tile_lists.reshape(seq_count, shard_tiles * top_count)
    need_out = jnp.any(by_run[:, :, None] == tile_ids[None, None, :], axis=1)
    slot_out = jnp.cumsum(need_out.astype(jnp.int32), axis=1) - 1
    slot_ids = jnp.arange(capacity, dtype=jnp.int32)
    pick_table = need_out[:, None, :] & (slot_out[:, None, :] == slot_ids[None, :, None])
    pick_table = pick_table.astype(jnp.bfloat16).reshape(seq_count * capacity, shard_tiles)
    own_lists = lax.dynamic_slice_in_dim(tile_lists, seq_index * shard_tiles, shard_tiles, 0)
    all_ids = jnp.arange(total_tiles, dtype=jnp.int32)
    matches = own_lists[:, :, None] == all_ids[None, None, :]
    listed = jnp.any(matches, axis=1).reshape(shard_tiles, seq_count, shard_tiles)
    need_in = jnp.any(listed, axis=0)
    slot_in = jnp.cumsum(need_in.astype(jnp.int32), axis=1) - 1
    queries_local, keys_local, values_local = (
        lax.all_to_all(queries, "head", split_axis=1, concat_axis=0, tiled=True),
        lax.all_to_all(keys, "head", split_axis=1, concat_axis=0, tiled=True),
        lax.all_to_all(values, "head", split_axis=1, concat_axis=0, tiled=True),
    )
    received = lax.all_to_all(
        select_slots(
            pick_table,
            (keys_local, values_local),
            seq_count,
            capacity,
            shard_tiles,
            tile_rows,
            local_heads,
            head_dim,
        ),
        "seq",
        split_axis=0,
        concat_axis=0,
        tiled=True,
    )
    key_slots = received[:, :, 0]
    value_slots = received[:, :, 1]
    flat_slots = jnp.broadcast_to(slot_in.reshape(1, 1, total_tiles), matches.shape)
    listed_slot = jnp.sum(jnp.where(matches, flat_slots, 0), axis=2)
    source_run = own_lists // shard_tiles
    slot_index = source_run * capacity + listed_slot
    query_tiles = queries_local.reshape(shard_tiles, tile_rows, local_heads, head_dim)
    slot_shape = (seq_count * capacity, local_heads, tile_rows, head_dim)
    key_flat = key_slots.reshape(slot_shape)
    value_flat = value_slots.reshape(slot_shape)

    def joined_tile(args):
        rounded, row_total = score_tile(key_flat, score_scale, args[0], args[1])
        return mix_tile(value_flat, rounded, row_total, args[1])

    attended = lax.map(joined_tile, (query_tiles, slot_index))
    attended = attended.reshape(local_rows, local_heads * head_dim)
    return lax.all_to_all(attended, "head", split_axis=0, concat_axis=1, tiled=True)


PLANES = 4
SIDE = 2
AXES = ("groups", "z", "y", "head")
RANKS = ("y", "head")
INWARD = [(0, 1), (3, 2)]
OUTWARD = [(1, 0), (2, 3)]
CROSS = [(1, 2), (2, 1)]
EXPONENT = HD**-0.5 * math.log2(math.e)
UNROLL = 4
COST = 9 * 10**9
LONG = 24 * 10**9
VMEM_LIMIT = 60 * 1024 * 1024


def shuffle_kernel(*refs, parts, source_count):
    sources, outs = refs[:source_count], refs[source_count : source_count + len(parts)]
    bufs, sems = refs[source_count + len(parts) : -1], refs[-1]
    loads, stores = {}, []
    for wanted in parts:
        for which, chunk in wanted:
            width = outs[0].shape[0] * HD
            columns = pl.ds(chunk * width, width)
            loads[which, chunk] = pltpu.make_async_copy(
                sources[which].at[:, columns], bufs[which].at[:, columns], sems.at[len(loads)]
            )
            loads[which, chunk].start()
    for out, wanted in zip(outs, parts):
        for at, (which, chunk) in enumerate(wanted):
            loads[which, chunk].wait()
            for lane in range(out.shape[0]):
                column = (chunk * out.shape[0] + lane) * HD
                store = pltpu.make_async_copy(
                    bufs[which].at[:, pl.ds(column, HD)],
                    out.at[lane, at],
                    sems.at[len(loads) + len(stores)],
                )
                store.start()
                stores.append(store)
    for store in stores:
        store.wait()


def shuffle(arrays, lanes, parts, name):
    rows = arrays[0].shape[0]
    kernel = functools.partial(shuffle_kernel, parts=parts, source_count=len(arrays))
    moved = sum(len(p) for p in parts)
    return pl.pallas_call(
        kernel,
        out_shape=[
            jax.ShapeDtypeStruct((lanes, len(p), rows, HD), arrays[0].dtype) for p in parts
        ],
        in_specs=[pl.BlockSpec(memory_space=pl.ANY)] * len(arrays),
        out_specs=[pl.BlockSpec(memory_space=pl.ANY)] * len(parts),
        scratch_shapes=[pltpu.VMEM(a.shape, a.dtype) for a in arrays]
        + [pltpu.SemaphoreType.DMA((moved * (lanes + 1),))],
        compiler_params=pltpu.CompilerParams(vmem_limit_bytes=VMEM_LIMIT),
        cost_estimate=pl.CostEstimate(
            flops=0, bytes_accessed=2 * moved * lanes * rows * HD * 2, transcendentals=0
        ),
        name=name,
    )(*arrays)


def gather_kernel(*refs):
    sources, out, buf, sems = refs[:-3], refs[-3], refs[-2], refs[-1]
    loads = []
    for source in sources:
        for at in range(source.shape[1]):
            for lane in range(source.shape[0]):
                column = pl.ds(len(loads) * HD, HD)
                load = pltpu.make_async_copy(
                    source.at[lane, at], buf.at[:, column], sems.at[len(loads)]
                )
                load.start()
                loads.append(load)
    for load in loads:
        load.wait()
    store = pltpu.make_async_copy(buf, out, sems.at[len(loads)])
    store.start()
    store.wait()


def gather_out(parts):
    rows = parts[0].shape[2]
    blocks = sum(p.shape[0] * p.shape[1] for p in parts)
    return pl.pallas_call(
        gather_kernel,
        out_shape=jax.ShapeDtypeStruct((rows, blocks * HD), parts[0].dtype),
        in_specs=[pl.BlockSpec(memory_space=pl.ANY)] * len(parts),
        out_specs=pl.BlockSpec(memory_space=pl.ANY),
        scratch_shapes=[
            pltpu.VMEM((rows, blocks * HD), parts[0].dtype),
            pltpu.SemaphoreType.DMA((blocks + 1,)),
        ],
        compiler_params=pltpu.CompilerParams(vmem_limit_bytes=VMEM_LIMIT),
        name="gather_out",
    )(*parts)


def attend_kernel(count, lists, query, *refs, chunk, ats):
    picks = refs[: 2 * PLANES]
    out, query_buf, key_buf, value_buf, score_buf, sems = refs[2 * PLANES :]
    lanes, _, shard_tiles = query.shape[:3]
    tiles = lanes * shard_tiles
    top_count = lists.shape[1]
    blank = jnp.zeros((TILE, HD), jnp.bfloat16)

    def beside(left, right):
        return jnp.concatenate([left, right], axis=1)

    @pl.when(count[0] > 0)
    def _():
        for lane in range(lanes):
            place = pl.ds(lane * shard_tiles, shard_tiles)
            pltpu.make_async_copy(query.at[lane, chunk], query_buf.at[place], sems.at[0]).start()
        for kind, buf in enumerate((key_buf, value_buf)):
            for slot in range(PLANES):
                source, at = picks[kind * PLANES + slot], ats[kind]
                for lane in range(lanes):
                    place = pl.ds((slot * lanes + lane) * shard_tiles, shard_tiles)
                    pltpu.make_async_copy(
                        source.at[lane, at], buf.at[place], sems.at[1 + kind]
                    ).start()
        pltpu.make_async_copy(query_buf, query_buf, sems.at[0]).wait()
        pltpu.make_async_copy(key_buf, key_buf, sems.at[1]).wait()

        def listed(buf, pair, t):
            return beside(buf[lists[2 * pair, t]], buf[lists[2 * pair + 1, t]])

        def score(pair, at):
            wide = jnp.concatenate(
                [beside(query_buf[2 * pair], blank), beside(blank, query_buf[2 * pair + 1])], axis=0
            )
            keys = jnp.concatenate([listed(key_buf, pair, t) for t in range(top_count)], axis=0)
            score_buf[at] = lax.dot_general(
                wide, keys, (((1,), (1,)), ((), ())), preferred_element_type=jnp.float32
            )

        def mix(pair, at):
            scores = score_buf[at]
            row_top = jnp.max(scores, axis=1, keepdims=True)
            weights = jnp.exp2((scores - row_top) * EXPONENT)
            row_total = jnp.sum(weights, axis=1, keepdims=True)
            values = jnp.concatenate([listed(value_buf, pair, t) for t in range(top_count)], axis=0)
            mixture = jnp.dot(
                weights.astype(jnp.bfloat16), values, preferred_element_type=jnp.float32
            )
            first = mixture[:TILE, :HD] / row_total[:TILE]
            second = mixture[TILE:, HD:] / row_total[TILE:]
            out[2 * pair] = first.astype(jnp.bfloat16)
            out[2 * pair + 1] = second.astype(jnp.bfloat16)

        score(0, 0)
        pltpu.make_async_copy(value_buf, value_buf, sems.at[2]).wait()

        unroll = math.gcd(tiles // 2, UNROLL)

        def step(at, carry):
            for sub in range(unroll):
                pair = at * unroll + sub
                score(jnp.minimum(pair + 1, tiles // 2 - 1), (sub + 1) % 2)
                mix(pair, sub % 2)
            return carry

        lax.fori_loop(0, tiles // 2 // unroll, step, 0)


def attend(count, lists, query, keys, values, ats, chunk, cost, name):
    tiles, top_count = lists.shape
    lanes = query.shape[0]
    shaped = (lanes, -1, tiles // lanes, TILE, HD)
    return pl.pallas_call(
        functools.partial(attend_kernel, chunk=chunk, ats=ats),
        out_shape=jax.ShapeDtypeStruct((tiles, TILE, HD), jnp.bfloat16),
        in_specs=[pl.BlockSpec(memory_space=pltpu.SMEM)] * 2
        + [pl.BlockSpec(memory_space=pl.ANY)] * (1 + 2 * PLANES),
        out_specs=pl.BlockSpec(memory_space=pltpu.VMEM),
        scratch_shapes=[
            pltpu.VMEM((tiles, TILE, HD), jnp.bfloat16),
            pltpu.VMEM((PLANES * tiles, TILE, HD), jnp.bfloat16),
            pltpu.VMEM((PLANES * tiles, TILE, HD), jnp.bfloat16),
            pltpu.VMEM((2, 2 * TILE, top_count * TILE), jnp.float32),
            pltpu.SemaphoreType.DMA((3,)),
        ],
        compiler_params=pltpu.CompilerParams(vmem_limit_bytes=VMEM_LIMIT),
        cost_estimate=pl.CostEstimate(flops=cost, bytes_accessed=1, transcendentals=0),
        name=name,
    )(count, lists, query.reshape(shaped), *[a.reshape(shaped) for a in (*keys, *values)])


def after(array, *others):
    return lax.optimization_barrier((array, *others))[0]


def relay_plan(queries, keys, values, tile_lists):
    z = lax.axis_index("z")
    lanes = SIDE * lax.axis_size("head")
    chunks = queries.shape[1] // (lanes * HD)
    plane_tiles = tile_lists.shape[0] // PLANES
    at_end = (z == 0) | (z == PLANES - 1)

    def swap(array):
        return lax.all_to_all(array, RANKS, split_axis=0, concat_axis=0, tiled=True)

    def send(array, pairs, name):
        with jax.named_scope(name):
            return lax.ppermute(array, "z", pairs)

    far = z >= PLANES // 2
    rows = jnp.stack(
        [
            lax.dynamic_slice_in_dim(tile_lists, z * plane_tiles, plane_tiles, 0),
            lax.dynamic_slice_in_dim(tile_lists, (z ^ 1) * plane_tiles, plane_tiles, 0),
        ]
    )
    plane = rows // plane_tiles
    plane = jnp.where(far, PLANES - 1 - plane, plane)
    near = jnp.where(far, PLANES - 1 - z, z)
    slot = jnp.where(plane < 2, plane ^ near, plane)
    lists = slot * plane_tiles + rows % plane_tiles
    count = jnp.where(at_end, 0, 1).astype(jnp.int32).reshape(1)

    (first,) = shuffle([keys, values], lanes, [[(0, 0), (1, 0)]], "shuffle_first")
    own_0 = swap(first)
    rest_1, rest_q0, rest_2, rest_q = shuffle(
        [queries, keys, values],
        lanes,
        [[(1, 1), (2, 1)], [(0, 0), (0, 1)], [(1, 2), (2, 2)], [(0, 2)]],
        "shuffle_rest",
    )
    in_0 = send(own_0, INWARD, "in_0")
    cross_0 = send(own_0, CROSS, "cross_0")
    own_1 = swap(after(rest_1, own_0))
    relay_0 = send(after(in_0, cross_0), CROSS, "relay_0")
    in_1 = send(after(own_1, in_0), INWARD, "in_1")
    cross_1 = send(after(own_1, cross_0), CROSS, "cross_1")
    asked_0 = swap(after(rest_q0, own_1, cross_0, in_0))
    in_q0 = send(after(asked_0, in_0), INWARD, "in_q0")
    own_2 = swap(after(rest_2, asked_0))
    relay_1 = send(after(in_1, relay_0), CROSS, "relay_1")
    in_2 = send(after(own_2, in_1), INWARD, "in_2")
    cross_2 = send(after(own_2, relay_0, cross_1), CROSS, "cross_2")
    asked = swap(after(rest_q, own_2))
    in_q = send(after(asked, in_q0), INWARD, "in_q")
    relay_2 = send(after(in_2, relay_1), CROSS, "relay_2")

    def one(at, chunk, query, pairs, place, cost=COST):
        name = f"attend_{chunk}{at}"
        return attend(count, lists[at], query, pairs, pairs, (0, 1), place, cost, name)

    def home(beside, chunk):
        return send(beside, OUTWARD, f"out_{chunk}")

    def finish(parts):
        mixed = []
        for own, home in parts:
            mixed.append(jnp.where(at_end, home, own).reshape(lanes, -1, HD))
        return mixed[0][:, None] if len(mixed) == 1 else jnp.stack(mixed, axis=1)

    pairs = [own_0, in_0, cross_0, relay_0]
    mine_0 = one(0, 0, asked_0, pairs, 0)
    theirs_0 = one(1, 0, after(in_q0, mine_0), pairs, 0)
    home_0 = home(theirs_0, 0)
    pairs = [own_1, in_1, cross_1, relay_1]
    mine_1 = one(0, 1, after(asked_0, theirs_0), pairs, 1)
    theirs_1 = one(1, 1, after(in_q0, mine_1), pairs, 1, LONG)
    home_1 = home(theirs_1, 1)
    mixed = finish([(mine_0, home_0), (mine_1, home_1)])
    early = swap(mixed)
    pairs = [own_2, in_2, cross_2, relay_2]
    theirs_2 = one(1, 2, after(in_q, theirs_1, mixed), pairs, 0, 1)
    mine_2 = one(0, 2, after(asked, theirs_2), pairs, 0, 1)
    late = swap(after(finish([(mine_2, home(theirs_2, 2))]), early))
    return gather_out([early, late])


def solution(mesh):
    seq_count, head_count = mesh.shape["seq"], mesh.shape["head"]
    if seq_count == PLANES * SIDE:
        planned = Mesh(mesh.devices.reshape(-1, PLANES, SIDE, head_count), AXES)
        plan, tokens = relay_plan, AXES
    else:
        planned, plan, tokens = mesh, slot_plan, ("groups", "seq", "head")
    placed = P(tokens, None)
    return jax.shard_map(
        plan,
        mesh=planned,
        in_specs=(placed, placed, placed, P("groups", None)),
        out_specs=placed,
        check_vma=False,
    )
```

```python
import functools
import math

import jax
import jax.numpy as jnp
from jax import lax
from jax.experimental import pallas as pl
from jax.experimental.pallas import tpu as pltpu
from jax.sharding import Mesh, PartitionSpec as P

HD = 128
TILE = 64


def score_tile(key_flat, score_scale, query_tile, row_index):
    gathered = key_flat[row_index]
    scores = (
        jnp.einsum("qhd,khtd->hqkt", query_tile, gathered, preferred_element_type=jnp.float32)
        * score_scale
    )
    row_top = jnp.max(scores, axis=(2, 3), keepdims=True)
    weights = jnp.exp(scores - row_top)
    row_total = jnp.sum(weights, axis=(2, 3))
    return (weights.astype(jnp.bfloat16), row_total)


def mix_tile(value_flat, rounded, row_total, row_index):
    gathered = value_flat[row_index]
    mixture = jnp.einsum("hqkt,khtd->qhd", rounded, gathered, preferred_element_type=jnp.float32)
    mixture = mixture / jnp.transpose(row_total)[:, :, None]
    return mixture.astype(jnp.bfloat16).reshape(mixture.shape[0], -1)


def select_slots(
    pick_table, arrays, seq_count, capacity, shard_tiles, tile_rows, local_heads, head_dim
):
    count = len(arrays)
    stacked = jnp.stack(arrays, 0).reshape(count, shard_tiles, tile_rows, local_heads, head_dim)
    stacked = stacked.transpose(1, 0, 3, 2, 4).reshape(shard_tiles, -1)
    outgoing = jnp.dot(pick_table, stacked, preferred_element_type=jnp.float32).astype(jnp.bfloat16)
    return outgoing.reshape(seq_count, capacity, count, local_heads, tile_rows, head_dim)


def slot_plan(queries, keys, values, tile_lists):
    seq_count = lax.axis_size("seq")
    head_count = lax.axis_size("head")
    head_dim = HD
    tile_rows = TILE
    total_tiles, top_count = tile_lists.shape
    local_heads = queries.shape[1] // head_dim // head_count
    local_rows = queries.shape[0] * head_count
    shard_tiles = local_rows // tile_rows
    capacity = 64 // seq_count
    seq_index = lax.axis_index("seq")
    score_scale = head_dim ** (-0.5)
    tile_ids = seq_index * shard_tiles + jnp.arange(shard_tiles, dtype=jnp.int32)
    by_run = tile_lists.reshape(seq_count, shard_tiles * top_count)
    need_out = jnp.any(by_run[:, :, None] == tile_ids[None, None, :], axis=1)
    slot_out = jnp.cumsum(need_out.astype(jnp.int32), axis=1) - 1
    slot_ids = jnp.arange(capacity, dtype=jnp.int32)
    pick_table = need_out[:, None, :] & (slot_out[:, None, :] == slot_ids[None, :, None])
    pick_table = pick_table.astype(jnp.bfloat16).reshape(seq_count * capacity, shard_tiles)
    own_lists = lax.dynamic_slice_in_dim(tile_lists, seq_index * shard_tiles, shard_tiles, 0)
    all_ids = jnp.arange(total_tiles, dtype=jnp.int32)
    matches = own_lists[:, :, None] == all_ids[None, None, :]
    listed = jnp.any(matches, axis=1).reshape(shard_tiles, seq_count, shard_tiles)
    need_in = jnp.any(listed, axis=0)
    slot_in = jnp.cumsum(need_in.astype(jnp.int32), axis=1) - 1
    queries_local, keys_local, values_local = (
        lax.all_to_all(queries, "head", split_axis=1, concat_axis=0, tiled=True),
        lax.all_to_all(keys, "head", split_axis=1, concat_axis=0, tiled=True),
        lax.all_to_all(values, "head", split_axis=1, concat_axis=0, tiled=True),
    )
    received = lax.all_to_all(
        select_slots(
            pick_table,
            (keys_local, values_local),
            seq_count,
            capacity,
            shard_tiles,
            tile_rows,
            local_heads,
            head_dim,
        ),
        "seq",
        split_axis=0,
        concat_axis=0,
        tiled=True,
    )
    key_slots = received[:, :, 0]
    value_slots = received[:, :, 1]
    flat_slots = jnp.broadcast_to(slot_in.reshape(1, 1, total_tiles), matches.shape)
    listed_slot = jnp.sum(jnp.where(matches, flat_slots, 0), axis=2)
    source_run = own_lists // shard_tiles
    slot_index = source_run * capacity + listed_slot
    query_tiles = queries_local.reshape(shard_tiles, tile_rows, local_heads, head_dim)
    slot_shape = (seq_count * capacity, local_heads, tile_rows, head_dim)
    key_flat = key_slots.reshape(slot_shape)
    value_flat = value_slots.reshape(slot_shape)

    def joined_tile(args):
        rounded, row_total = score_tile(key_flat, score_scale, args[0], args[1])
        return mix_tile(value_flat, rounded, row_total, args[1])

    attended = lax.map(joined_tile, (query_tiles, slot_index))
    attended = attended.reshape(local_rows, local_heads * head_dim)
    return lax.all_to_all(attended, "head", split_axis=0, concat_axis=1, tiled=True)


PLANES = 4
SIDE = 2
AXES = ("groups", "z", "y", "head")
RANKS = ("y", "head")
INWARD = [(0, 1), (3, 2)]
OUTWARD = [(1, 0), (2, 3)]
CROSS = [(1, 2), (2, 1)]
EXPONENT = HD**-0.5 * math.log2(math.e)
UNROLL = 4
COST = 9 * 10**9
LONG = 24 * 10**9
VMEM_LIMIT = 60 * 1024 * 1024


def shuffle_kernel(*refs, parts, source_count):
    sources, outs = refs[:source_count], refs[source_count : source_count + len(parts)]
    bufs, sems = refs[source_count + len(parts) : -1], refs[-1]
    loads, stores = {}, []
    for wanted in parts:
        for which, chunk in wanted:
            width = outs[0].shape[0] * HD
            columns = pl.ds(chunk * width, width)
            loads[which, chunk] = pltpu.make_async_copy(
                sources[which].at[:, columns], bufs[which].at[:, columns], sems.at[len(loads)]
            )
            loads[which, chunk].start()
    for out, wanted in zip(outs, parts):
        for at, (which, chunk) in enumerate(wanted):
            loads[which, chunk].wait()
            for lane in range(out.shape[0]):
                column = (chunk * out.shape[0] + lane) * HD
                store = pltpu.make_async_copy(
                    bufs[which].at[:, pl.ds(column, HD)],
                    out.at[lane, at],
                    sems.at[len(loads) + len(stores)],
                )
                store.start()
                stores.append(store)
    for store in stores:
        store.wait()


def shuffle(arrays, lanes, parts, name):
    rows = arrays[0].shape[0]
    kernel = functools.partial(shuffle_kernel, parts=parts, source_count=len(arrays))
    moved = sum(len(p) for p in parts)
    return pl.pallas_call(
        kernel,
        out_shape=[
            jax.ShapeDtypeStruct((lanes, len(p), rows, HD), arrays[0].dtype) for p in parts
        ],
        in_specs=[pl.BlockSpec(memory_space=pl.ANY)] * len(arrays),
        out_specs=[pl.BlockSpec(memory_space=pl.ANY)] * len(parts),
        scratch_shapes=[pltpu.VMEM(a.shape, a.dtype) for a in arrays]
        + [pltpu.SemaphoreType.DMA((moved * (lanes + 1),))],
        compiler_params=pltpu.CompilerParams(vmem_limit_bytes=VMEM_LIMIT),
        cost_estimate=pl.CostEstimate(
            flops=0, bytes_accessed=2 * moved * lanes * rows * HD * 2, transcendentals=0
        ),
        name=name,
    )(*arrays)


def gather_kernel(*refs, first, held):
    sources, out, buf, sems = refs[: len(refs) - 3 - held], refs[-3], refs[-2], refs[-1]
    moves = []
    for source in sources:
        for at in range(source.shape[1]):
            for lane in range(source.shape[0]):
                here = pl.ds(len(moves) * HD, HD)
                there = pl.ds((first + len(moves)) * HD, HD)
                load = pltpu.make_async_copy(
                    source.at[lane, at], buf.at[:, here], sems.at[0, len(moves)]
                )
                load.start()
                store = pltpu.make_async_copy(
                    buf.at[:, here], out.at[:, there], sems.at[1, len(moves)]
                )
                moves.append((load, store))
    for load, store in moves:
        load.wait()
        store.start()
    for load, store in moves:
        store.wait()


def gather_out(parts, first, total, held, name):
    rows = parts[0].shape[2]
    blocks = sum(p.shape[0] * p.shape[1] for p in parts)
    given = [] if held is None else [held]
    return pl.pallas_call(
        functools.partial(gather_kernel, first=first, held=len(given)),
        out_shape=jax.ShapeDtypeStruct((rows, total * HD), parts[0].dtype),
        in_specs=[pl.BlockSpec(memory_space=pl.ANY)] * (len(parts) + len(given)),
        out_specs=pl.BlockSpec(memory_space=pl.ANY),
        scratch_shapes=[
            pltpu.VMEM((rows, blocks * HD), parts[0].dtype),
            pltpu.SemaphoreType.DMA((2, blocks)),
        ],
        input_output_aliases={len(parts): 0} if given else {},
        compiler_params=pltpu.CompilerParams(vmem_limit_bytes=VMEM_LIMIT),
        cost_estimate=pl.CostEstimate(flops=1, bytes_accessed=1, transcendentals=0),
        name=name,
    )(*parts, *given)


def attend_kernel(count, lists, query, *refs, chunk, ats):
    picks = refs[: 2 * PLANES]
    out, query_buf, key_buf, value_buf, score_buf, sems = refs[2 * PLANES :]
    lanes, _, shard_tiles = query.shape[:3]
    tiles = lanes * shard_tiles
    top_count = lists.shape[1]
    blank = jnp.zeros((TILE, HD), jnp.bfloat16)

    def beside(left, right):
        return jnp.concatenate([left, right], axis=1)

    @pl.when(count[0] > 0)
    def _():
        shaped = (lanes, shard_tiles, TILE, HD)
        pltpu.make_async_copy(query.at[:, chunk], query_buf.reshape(shaped), sems.at[0]).start()
        for kind, buf in enumerate((key_buf, value_buf)):
            for slot in range(PLANES):
                pltpu.make_async_copy(
                    picks[kind * PLANES + slot].at[:, ats[kind]],
                    buf.reshape((PLANES, *shaped)).at[slot],
                    sems.at[1 + kind],
                ).start()
        pltpu.make_async_copy(query_buf, query_buf, sems.at[0]).wait()
        pltpu.make_async_copy(key_buf, key_buf, sems.at[1]).wait()

        def listed(buf, pair, t):
            return beside(buf[lists[2 * pair, t]], buf[lists[2 * pair + 1, t]])

        def score(pair, at):
            wide = jnp.concatenate(
                [beside(query_buf[2 * pair], blank), beside(blank, query_buf[2 * pair + 1])], axis=0
            )
            keys = jnp.concatenate([listed(key_buf, pair, t) for t in range(top_count)], axis=0)
            score_buf[at] = lax.dot_general(
                wide, keys, (((1,), (1,)), ((), ())), preferred_element_type=jnp.float32
            )

        def mix(pair, at):
            scores = score_buf[at]
            row_top = jnp.max(scores, axis=1, keepdims=True)
            weights = jnp.exp2((scores - row_top) * EXPONENT)
            row_total = jnp.sum(weights, axis=1, keepdims=True)
            values = jnp.concatenate([listed(value_buf, pair, t) for t in range(top_count)], axis=0)
            mixture = jnp.dot(
                weights.astype(jnp.bfloat16), values, preferred_element_type=jnp.float32
            )
            first = mixture[:TILE, :HD] / row_total[:TILE]
            second = mixture[TILE:, HD:] / row_total[TILE:]
            out[2 * pair] = first.astype(jnp.bfloat16)
            out[2 * pair + 1] = second.astype(jnp.bfloat16)

        score(0, 0)
        pltpu.make_async_copy(value_buf, value_buf, sems.at[2]).wait()

        unroll = math.gcd(tiles // 2, UNROLL)

        def step(at, carry):
            for sub in range(unroll):
                pair = at * unroll + sub
                score(jnp.minimum(pair + 1, tiles // 2 - 1), (sub + 1) % 2)
                mix(pair, sub % 2)
            return carry

        lax.fori_loop(0, tiles // 2 // unroll, step, 0)


def attend(count, lists, query, keys, values, ats, chunk, cost, name):
    tiles, top_count = lists.shape
    lanes = query.shape[0]
    shaped = (lanes, -1, tiles // lanes, TILE, HD)
    return pl.pallas_call(
        functools.partial(attend_kernel, chunk=chunk, ats=ats),
        out_shape=jax.ShapeDtypeStruct((tiles, TILE, HD), jnp.bfloat16),
        in_specs=[pl.BlockSpec(memory_space=pltpu.SMEM)] * 2
        + [pl.BlockSpec(memory_space=pl.ANY)] * (1 + 2 * PLANES),
        out_specs=pl.BlockSpec(memory_space=pltpu.VMEM),
        scratch_shapes=[
            pltpu.VMEM((tiles, TILE, HD), jnp.bfloat16),
            pltpu.VMEM((PLANES * tiles, TILE, HD), jnp.bfloat16),
            pltpu.VMEM((PLANES * tiles, TILE, HD), jnp.bfloat16),
            pltpu.VMEM((2, 2 * TILE, top_count * TILE), jnp.float32),
            pltpu.SemaphoreType.DMA((3,)),
        ],
        compiler_params=pltpu.CompilerParams(vmem_limit_bytes=VMEM_LIMIT),
        cost_estimate=pl.CostEstimate(flops=cost, bytes_accessed=1, transcendentals=0),
        name=name,
    )(count, lists, query.reshape(shaped), *[a.reshape(shaped) for a in (*keys, *values)])


def after(array, *others):
    return lax.optimization_barrier((array, *others))[0]


def relay_plan(queries, keys, values, tile_lists):
    z = lax.axis_index("z")
    lanes = SIDE * lax.axis_size("head")
    chunks = queries.shape[1] // (lanes * HD)
    plane_tiles = tile_lists.shape[0] // PLANES
    at_end = (z == 0) | (z == PLANES - 1)

    def swap(array):
        return lax.all_to_all(array, RANKS, split_axis=0, concat_axis=0, tiled=True)

    def send(array, pairs, name):
        with jax.named_scope(name):
            return lax.ppermute(array, "z", pairs)

    far = z >= PLANES // 2
    rows = jnp.stack(
        [
            lax.dynamic_slice_in_dim(tile_lists, z * plane_tiles, plane_tiles, 0),
            lax.dynamic_slice_in_dim(tile_lists, (z ^ 1) * plane_tiles, plane_tiles, 0),
        ]
    )
    plane = rows // plane_tiles
    plane = jnp.where(far, PLANES - 1 - plane, plane)
    near = jnp.where(far, PLANES - 1 - z, z)
    slot = jnp.where(plane < 2, plane ^ near, plane)
    lists = slot * plane_tiles + rows % plane_tiles
    count = jnp.where(at_end, 0, 1).astype(jnp.int32).reshape(1)

    first, rest_2 = shuffle(
        [keys, values], lanes, [[(0, 0), (1, 0)], [(0, 2), (1, 2)]], "shuffle_first"
    )
    raw_2 = send(rest_2, CROSS, "cross_raw_2")
    own_0 = swap(first)
    rest_1, rest_q0, rest_q = shuffle(
        [queries, keys, values],
        lanes,
        [[(1, 1), (2, 1)], [(0, 0)], [(0, 1), (0, 2)]],
        "shuffle_rest",
    )
    in_0 = send(own_0, INWARD, "in_0")
    cross_0 = send(own_0, CROSS, "cross_0")
    own_1 = swap(after(rest_1, own_0, raw_2))
    relay_0 = send(after(in_0, cross_0), CROSS, "relay_0")
    in_1 = send(after(own_1, in_0), INWARD, "in_1")
    cross_1 = send(after(own_1, cross_0), CROSS, "cross_1")
    asked_0 = swap(after(rest_q0, own_1, cross_0, in_0))
    in_q0 = send(after(asked_0, in_0), INWARD, "in_q0")
    own_2 = swap(after(rest_2, asked_0))
    relay_1 = send(after(in_1, relay_0), CROSS, "relay_1")
    in_2 = send(after(own_2, in_1), INWARD, "in_2")
    asked = swap(after(rest_q, own_2))
    in_q = send(after(asked, in_q0), INWARD, "in_q")
    cross_2 = swap(after(raw_2, asked))
    relay_2 = send(after(in_2, cross_1), CROSS, "relay_2")

    def one(at, chunk, query, pairs, place, cost=COST):
        name = f"attend_{chunk}{at}"
        return attend(count, lists[at], query, pairs, pairs, (0, 1), place, cost, name)

    def home(beside, chunk):
        return send(beside, OUTWARD, f"out_{chunk}")

    def finish(parts):
        mixed = []
        for own, home in parts:
            mixed.append(jnp.where(at_end, home, own).reshape(lanes, -1, HD))
        return mixed[0][:, None] if len(mixed) == 1 else jnp.stack(mixed, axis=1)

    pairs = [own_0, in_0, cross_0, relay_0]
    mine_0 = one(0, 0, asked_0, pairs, 0)
    theirs_0 = one(1, 0, after(in_q0, mine_0), pairs, 0)
    home_0 = home(theirs_0, 0)
    pairs = [own_1, in_1, cross_1, relay_1]
    mine_1 = one(0, 1, after(asked, theirs_0, cross_2), pairs, 0)
    theirs_1 = one(1, 1, after(in_q, mine_1), pairs, 0, LONG)
    home_1 = home(theirs_1, 1)
    pairs = [own_2, in_2, cross_2, relay_2]
    theirs_2 = one(1, 2, after(in_q, theirs_1), pairs, 1, 1)
    mixed = finish([(mine_0, home_0), (mine_1, after(home_1, theirs_2))])
    early = swap(mixed)
    mine_2 = one(0, 2, after(asked, theirs_2), pairs, 1, 1)
    late = swap(after(finish([(mine_2, home(theirs_2, 2))]), early))
    return gather_out([early, late], 0, chunks * lanes, None, "gather_out")


def solution(mesh):
    seq_count, head_count = mesh.shape["seq"], mesh.shape["head"]
    if seq_count == PLANES * SIDE:
        planned = Mesh(mesh.devices.reshape(-1, PLANES, SIDE, head_count), AXES)
        plan, tokens = relay_plan, AXES
    else:
        planned, plan, tokens = mesh, slot_plan, ("groups", "seq", "head")
    placed = P(tokens, None)
    return jax.shard_map(
        plan,
        mesh=planned,
        in_specs=(placed, placed, placed, P("groups", None)),
        out_specs=placed,
        check_vma=False,
    )
```

```python
import functools
import math

import jax
import jax.numpy as jnp
from jax import lax
from jax.experimental import pallas as pl
from jax.experimental.pallas import tpu as pltpu
from jax.sharding import Mesh, PartitionSpec as P

HD = 128
TILE = 64


def score_tile(key_flat, score_scale, query_tile, row_index):
    gathered = key_flat[row_index]
    scores = (
        jnp.einsum("qhd,khtd->hqkt", query_tile, gathered, preferred_element_type=jnp.float32)
        * score_scale
    )
    row_top = jnp.max(scores, axis=(2, 3), keepdims=True)
    weights = jnp.exp(scores - row_top)
    row_total = jnp.sum(weights, axis=(2, 3))
    return (weights.astype(jnp.bfloat16), row_total)


def mix_tile(value_flat, rounded, row_total, row_index):
    gathered = value_flat[row_index]
    mixture = jnp.einsum("hqkt,khtd->qhd", rounded, gathered, preferred_element_type=jnp.float32)
    mixture = mixture / jnp.transpose(row_total)[:, :, None]
    return mixture.astype(jnp.bfloat16).reshape(mixture.shape[0], -1)


def select_slots(
    pick_table, arrays, seq_count, capacity, shard_tiles, tile_rows, local_heads, head_dim
):
    count = len(arrays)
    stacked = jnp.stack(arrays, 0).reshape(count, shard_tiles, tile_rows, local_heads, head_dim)
    stacked = stacked.transpose(1, 0, 3, 2, 4).reshape(shard_tiles, -1)
    outgoing = jnp.dot(pick_table, stacked, preferred_element_type=jnp.float32).astype(jnp.bfloat16)
    return outgoing.reshape(seq_count, capacity, count, local_heads, tile_rows, head_dim)


def slot_plan(queries, keys, values, tile_lists):
    seq_count = lax.axis_size("seq")
    head_count = lax.axis_size("head")
    head_dim = HD
    tile_rows = TILE
    total_tiles, top_count = tile_lists.shape
    local_heads = queries.shape[1] // head_dim // head_count
    local_rows = queries.shape[0] * head_count
    shard_tiles = local_rows // tile_rows
    capacity = 64 // seq_count
    seq_index = lax.axis_index("seq")
    score_scale = head_dim ** (-0.5)
    tile_ids = seq_index * shard_tiles + jnp.arange(shard_tiles, dtype=jnp.int32)
    by_run = tile_lists.reshape(seq_count, shard_tiles * top_count)
    need_out = jnp.any(by_run[:, :, None] == tile_ids[None, None, :], axis=1)
    slot_out = jnp.cumsum(need_out.astype(jnp.int32), axis=1) - 1
    slot_ids = jnp.arange(capacity, dtype=jnp.int32)
    pick_table = need_out[:, None, :] & (slot_out[:, None, :] == slot_ids[None, :, None])
    pick_table = pick_table.astype(jnp.bfloat16).reshape(seq_count * capacity, shard_tiles)
    own_lists = lax.dynamic_slice_in_dim(tile_lists, seq_index * shard_tiles, shard_tiles, 0)
    all_ids = jnp.arange(total_tiles, dtype=jnp.int32)
    matches = own_lists[:, :, None] == all_ids[None, None, :]
    listed = jnp.any(matches, axis=1).reshape(shard_tiles, seq_count, shard_tiles)
    need_in = jnp.any(listed, axis=0)
    slot_in = jnp.cumsum(need_in.astype(jnp.int32), axis=1) - 1
    queries_local, keys_local, values_local = (
        lax.all_to_all(queries, "head", split_axis=1, concat_axis=0, tiled=True),
        lax.all_to_all(keys, "head", split_axis=1, concat_axis=0, tiled=True),
        lax.all_to_all(values, "head", split_axis=1, concat_axis=0, tiled=True),
    )
    received = lax.all_to_all(
        select_slots(
            pick_table,
            (keys_local, values_local),
            seq_count,
            capacity,
            shard_tiles,
            tile_rows,
            local_heads,
            head_dim,
        ),
        "seq",
        split_axis=0,
        concat_axis=0,
        tiled=True,
    )
    key_slots = received[:, :, 0]
    value_slots = received[:, :, 1]
    flat_slots = jnp.broadcast_to(slot_in.reshape(1, 1, total_tiles), matches.shape)
    listed_slot = jnp.sum(jnp.where(matches, flat_slots, 0), axis=2)
    source_run = own_lists // shard_tiles
    slot_index = source_run * capacity + listed_slot
    query_tiles = queries_local.reshape(shard_tiles, tile_rows, local_heads, head_dim)
    slot_shape = (seq_count * capacity, local_heads, tile_rows, head_dim)
    key_flat = key_slots.reshape(slot_shape)
    value_flat = value_slots.reshape(slot_shape)

    def joined_tile(args):
        rounded, row_total = score_tile(key_flat, score_scale, args[0], args[1])
        return mix_tile(value_flat, rounded, row_total, args[1])

    attended = lax.map(joined_tile, (query_tiles, slot_index))
    attended = attended.reshape(local_rows, local_heads * head_dim)
    return lax.all_to_all(attended, "head", split_axis=0, concat_axis=1, tiled=True)


PLANES = 4
SIDE = 2
AXES = ("groups", "z", "y", "head")
RANKS = ("y", "head")
SWAP = [(0, 1), (1, 0), (2, 3), (3, 2)]
INWARD = [(0, 1), (3, 2)]
OUTWARD = [(1, 0), (2, 3)]
CROSS = [(1, 2), (2, 1)]
EXPONENT = HD**-0.5 * math.log2(math.e)
UNROLL = 4
COST = 9 * 10**9
LONG = 24 * 10**9
VMEM_LIMIT = 60 * 1024 * 1024


def shuffle_kernel(*refs, parts, source_count):
    sources, outs = refs[:source_count], refs[source_count : source_count + len(parts)]
    bufs, sems = refs[source_count + len(parts) : -1], refs[-1]
    loads, stores = {}, []
    for wanted in parts:
        for which, chunk in wanted:
            width = outs[0].shape[0] * HD
            columns = pl.ds(chunk * width, width)
            loads[which, chunk] = pltpu.make_async_copy(
                sources[which].at[:, columns], bufs[which].at[:, columns], sems.at[len(loads)]
            )
            loads[which, chunk].start()
    for out, wanted in zip(outs, parts):
        for at, (which, chunk) in enumerate(wanted):
            loads[which, chunk].wait()
            for lane in range(out.shape[0]):
                column = (chunk * out.shape[0] + lane) * HD
                store = pltpu.make_async_copy(
                    bufs[which].at[:, pl.ds(column, HD)],
                    out.at[lane, at],
                    sems.at[len(loads) + len(stores)],
                )
                store.start()
                stores.append(store)
    for store in stores:
        store.wait()


def shuffle(arrays, lanes, parts, name):
    rows = arrays[0].shape[0]
    kernel = functools.partial(shuffle_kernel, parts=parts, source_count=len(arrays))
    moved = sum(len(p) for p in parts)
    return pl.pallas_call(
        kernel,
        out_shape=[
            jax.ShapeDtypeStruct((lanes, len(p), rows, HD), arrays[0].dtype) for p in parts
        ],
        in_specs=[pl.BlockSpec(memory_space=pl.ANY)] * len(arrays),
        out_specs=[pl.BlockSpec(memory_space=pl.ANY)] * len(parts),
        scratch_shapes=[pltpu.VMEM(a.shape, a.dtype) for a in arrays]
        + [pltpu.SemaphoreType.DMA((moved * (lanes + 1),))],
        compiler_params=pltpu.CompilerParams(vmem_limit_bytes=VMEM_LIMIT),
        cost_estimate=pl.CostEstimate(
            flops=0, bytes_accessed=2 * moved * lanes * rows * HD * 2, transcendentals=0
        ),
        name=name,
    )(*arrays)


def gather_kernel(*refs, first, held):
    sources, out, buf, sems = refs[: len(refs) - 3 - held], refs[-3], refs[-2], refs[-1]
    moves = []
    for source in sources:
        for at in range(source.shape[1]):
            for lane in range(source.shape[0]):
                here = pl.ds(len(moves) * HD, HD)
                there = pl.ds((first + len(moves)) * HD, HD)
                load = pltpu.make_async_copy(
                    source.at[lane, at], buf.at[:, here], sems.at[0, len(moves)]
                )
                load.start()
                store = pltpu.make_async_copy(
                    buf.at[:, here], out.at[:, there], sems.at[1, len(moves)]
                )
                moves.append((load, store))
    for load, store in moves:
        load.wait()
        store.start()
    for load, store in moves:
        store.wait()


def gather_out(parts, first, total, held, name):
    rows = parts[0].shape[2]
    blocks = sum(p.shape[0] * p.shape[1] for p in parts)
    given = [] if held is None else [held]
    return pl.pallas_call(
        functools.partial(gather_kernel, first=first, held=len(given)),
        out_shape=jax.ShapeDtypeStruct((rows, total * HD), parts[0].dtype),
        in_specs=[pl.BlockSpec(memory_space=pl.ANY)] * (len(parts) + len(given)),
        out_specs=pl.BlockSpec(memory_space=pl.ANY),
        scratch_shapes=[
            pltpu.VMEM((rows, blocks * HD), parts[0].dtype),
            pltpu.SemaphoreType.DMA((2, blocks)),
        ],
        input_output_aliases={len(parts): 0} if given else {},
        compiler_params=pltpu.CompilerParams(vmem_limit_bytes=VMEM_LIMIT),
        cost_estimate=pl.CostEstimate(flops=1, bytes_accessed=1, transcendentals=0),
        name=name,
    )(*parts, *given)


def attend_kernel(flags, lists, query, *refs, chunk, ats, forwarded):
    out, query_buf, key_buf, value_buf, score_buf, sems = refs[-6:]
    lanes, _, shard_tiles = query.shape[:3]
    tiles = lanes * shard_tiles
    top_count = lists.shape[1]
    blank = jnp.zeros((TILE, HD), jnp.bfloat16)

    def beside(left, right):
        return jnp.concatenate([left, right], axis=1)

    @pl.when(flags[0] != 0)
    def _():
        shaped = (lanes, shard_tiles, TILE, HD)
        pltpu.make_async_copy(query.at[:, chunk], query_buf.reshape(shaped), sems.at[0]).start()
        def load(which, kind, slot):
            buf = (key_buf, value_buf)[kind]
            pltpu.make_async_copy(
                refs[which].at[:, ats[which]],
                buf.reshape((PLANES, *shaped)).at[slot],
                sems.at[1 + kind],
            ).start()

        for kind in range(2):
            for slot in range(PLANES if forwarded == 0 else PLANES - forwarded):
                load(kind * PLANES + slot, kind, slot)

        if forwarded > 0:

            @pl.when(flags[1] == 0)
            def _():
                for kind in range(2):
                    for slot in range(PLANES - forwarded, PLANES):
                        load(kind * PLANES + slot, kind, slot)

            @pl.when(flags[1] != 0)
            def _():
                for kind in range(2):
                    for at in range(forwarded):
                        which = 2 * PLANES + kind * forwarded + at
                        load(which, kind, PLANES - forwarded + at)

        pltpu.make_async_copy(query_buf, query_buf, sems.at[0]).wait()
        pltpu.make_async_copy(key_buf, key_buf, sems.at[1]).wait()

        def listed(buf, pair, t):
            return beside(buf[lists[2 * pair, t]], buf[lists[2 * pair + 1, t]])

        def score(pair, at):
            wide = jnp.concatenate(
                [beside(query_buf[2 * pair], blank), beside(blank, query_buf[2 * pair + 1])], axis=0
            )
            keys = jnp.concatenate([listed(key_buf, pair, t) for t in range(top_count)], axis=0)
            score_buf[at] = lax.dot_general(
                wide, keys, (((1,), (1,)), ((), ())), preferred_element_type=jnp.float32
            )

        def mix(pair, at):
            scores = score_buf[at]
            row_top = jnp.max(scores, axis=1, keepdims=True)
            weights = jnp.exp2((scores - row_top) * EXPONENT)
            row_total = jnp.sum(weights, axis=1, keepdims=True)
            values = jnp.concatenate([listed(value_buf, pair, t) for t in range(top_count)], axis=0)
            mixture = jnp.dot(
                weights.astype(jnp.bfloat16), values, preferred_element_type=jnp.float32
            )
            first = mixture[:TILE, :HD] / row_total[:TILE]
            second = mixture[TILE:, HD:] / row_total[TILE:]
            out[2 * pair] = first.astype(jnp.bfloat16)
            out[2 * pair + 1] = second.astype(jnp.bfloat16)

        score(0, 0)
        pltpu.make_async_copy(value_buf, value_buf, sems.at[2]).wait()

        unroll = math.gcd(tiles // 2, UNROLL)

        def step(at, carry):
            for sub in range(unroll):
                pair = at * unroll + sub
                score(jnp.minimum(pair + 1, tiles // 2 - 1), (sub + 1) % 2)
                mix(pair, sub % 2)
            return carry

        lax.fori_loop(0, tiles // 2 // unroll, step, 0)


def attend(flags, lists, query, keys, values, ats, chunk, cost, name):
    tiles, top_count = lists.shape
    lanes = query.shape[0]
    shaped = (lanes, -1, tiles // lanes, TILE, HD)
    forwarded = len(keys) - PLANES
    picks = [*keys[:PLANES], *values[:PLANES], *keys[PLANES:], *values[PLANES:]]
    return pl.pallas_call(
        functools.partial(attend_kernel, chunk=chunk, ats=ats, forwarded=forwarded),
        out_shape=jax.ShapeDtypeStruct((tiles, TILE, HD), jnp.bfloat16),
        in_specs=[pl.BlockSpec(memory_space=pltpu.SMEM)] * 2
        + [pl.BlockSpec(memory_space=pl.ANY)] * (1 + len(picks)),
        out_specs=pl.BlockSpec(memory_space=pltpu.VMEM),
        scratch_shapes=[
            pltpu.VMEM((tiles, TILE, HD), jnp.bfloat16),
            pltpu.VMEM((PLANES * tiles, TILE, HD), jnp.bfloat16),
            pltpu.VMEM((PLANES * tiles, TILE, HD), jnp.bfloat16),
            pltpu.VMEM((2, 2 * TILE, top_count * TILE), jnp.float32),
            pltpu.SemaphoreType.DMA((3,)),
        ],
        compiler_params=pltpu.CompilerParams(vmem_limit_bytes=VMEM_LIMIT),
        cost_estimate=pl.CostEstimate(flops=cost, bytes_accessed=1, transcendentals=0),
        name=name,
    )(flags, lists, query.reshape(shaped), *[a.reshape(shaped) for a in picks])


def after(array, *others):
    return lax.optimization_barrier((array, *others))[0]


def relay_plan(queries, keys, values, tile_lists):
    z = lax.axis_index("z")
    lanes = SIDE * lax.axis_size("head")
    chunks = queries.shape[1] // (lanes * HD)
    plane_tiles = tile_lists.shape[0] // PLANES
    at_end = (z == 0) | (z == PLANES - 1)

    def swap(array):
        return lax.all_to_all(array, RANKS, split_axis=0, concat_axis=0, tiled=True)

    def send(array, pairs, name):
        with jax.named_scope(name):
            return lax.ppermute(array, "z", pairs)

    far = z >= PLANES // 2
    rows = jnp.stack(
        [
            lax.dynamic_slice_in_dim(tile_lists, z * plane_tiles, plane_tiles, 0),
            lax.dynamic_slice_in_dim(tile_lists, (z ^ 1) * plane_tiles, plane_tiles, 0),
        ]
    )
    plane = rows // plane_tiles
    plane = jnp.where(far, PLANES - 1 - plane, plane)
    near = jnp.where(far, PLANES - 1 - z, z)
    slot = jnp.where(plane < 2, plane ^ near, plane)
    lists = slot * plane_tiles + rows % plane_tiles
    ends = at_end.astype(jnp.int32)
    inner, everyone = jnp.stack([1 - ends, 0 * ends]), jnp.stack([0 * ends + 1, ends])

    first, rest_2 = shuffle(
        [keys, values], lanes, [[(0, 0), (1, 0)], [(0, 2), (1, 2)]], "shuffle_first"
    )
    raw_2 = send(rest_2, CROSS, "cross_raw_2")
    own_0 = swap(first)
    rest_1, rest_q = shuffle(
        [queries, keys, values],
        lanes,
        [[(1, 1), (2, 1)], [(0, c) for c in range(chunks)]],
        "shuffle_rest",
    )
    in_0 = send(own_0, SWAP, "in_0")
    cross_0 = send(own_0, CROSS, "cross_0")
    own_1 = swap(after(rest_1, own_0, raw_2))
    relay_0 = send(after(in_0, cross_0), CROSS, "relay_0")
    in_1 = send(after(own_1, in_0), INWARD, "in_1")
    cross_1 = send(after(own_1, cross_0), CROSS, "cross_1")
    out_cross = send(cross_0, OUTWARD, "out_cross_0")
    own_2 = swap(after(rest_2, own_1, cross_0, in_0))
    out_relay = send(relay_0, OUTWARD, "out_relay_0")
    relay_1 = send(after(in_1, relay_0, out_cross), CROSS, "relay_1")
    in_2 = send(after(own_2, in_1), INWARD, "in_2")
    asked = swap(after(rest_q, own_2))
    in_q = send(after(asked[:, 1:], in_1), INWARD, "in_q")
    cross_2 = swap(after(raw_2, asked))
    relay_2 = send(after(in_2, cross_1), CROSS, "relay_2")

    def one(at, chunk, query, pairs, place, cost=COST):
        name = f"attend_{chunk}{at}"
        ats = ((0,) * PLANES + (1,) * PLANES) + (0,) * (len(pairs) - PLANES) + (1,) * (len(pairs) - PLANES)
        flags = inner if len(pairs) == PLANES else everyone
        return attend(flags, lists[at], query, pairs, pairs, ats, place, cost, name)

    def home(beside, chunk):
        return send(beside, OUTWARD, f"out_{chunk}")

    def finish(parts):
        mixed = []
        for own, home in parts:
            mixed.append(jnp.where(at_end, home, own).reshape(lanes, -1, HD))
        return mixed[0][:, None] if len(mixed) == 1 else jnp.stack(mixed, axis=1)

    pairs = [own_0, in_0, cross_0, relay_0, out_cross, out_relay]
    mine_0 = one(0, 0, asked, pairs, 0)
    early_0 = swap(mine_0.reshape(lanes, 1, -1, HD))
    pairs = [own_1, in_1, cross_1, relay_1]
    mine_1 = one(0, 1, after(asked, mine_0, cross_2), pairs, 1)
    theirs_1 = one(1, 1, after(in_q, mine_1), pairs, 0, LONG)
    home_1 = home(theirs_1, 1)
    pairs = [own_2, in_2, cross_2, relay_2]
    theirs_2 = one(1, 2, after(in_q, theirs_1, early_0), pairs, 1, 1)
    early = swap(after(finish([(mine_1, after(home_1, theirs_2))]), early_0))
    mine_2 = one(0, 2, after(asked, theirs_2), pairs, 2, 1)
    late = swap(after(finish([(mine_2, home(theirs_2, 2))]), early))
    return gather_out([early_0, early, late], 0, chunks * lanes, None, "gather_out")


def solution(mesh):
    seq_count, head_count = mesh.shape["seq"], mesh.shape["head"]
    if seq_count == PLANES * SIDE:
        planned = Mesh(mesh.devices.reshape(-1, PLANES, SIDE, head_count), AXES)
        plan, tokens = relay_plan, AXES
    else:
        planned, plan, tokens = mesh, slot_plan, ("groups", "seq", "head")
    placed = P(tokens, None)
    return jax.shard_map(
        plan,
        mesh=planned,
        in_specs=(placed, placed, placed, P("groups", None)),
        out_specs=placed,
        check_vma=False,
    )
```
